256 devices in a mesh: district: 16 (over x, z_hi), tile: 16 (over z_lo, y, core).
Axes of the slice: x: 4, y: 4, z: 8 (z_hi: 4, z_lo: 2; z = z_hi * 2 + z_lo), core: 2. Of those that a mesh axis runs over, the one named last changes fastest.
Arguments:
- parent_state: float32 [3, 256, 2048], P(None, 'district', 'tile'), may hold values from -6 to 6
- parent_depth: float32 [256, 2048], P('district', 'tile'), may hold values from 0.25 to 1
- child_state: float32 [3, 1024, 2048], P(None, 'district', 'tile'), may hold values from -6 to 6
- child_depth: float32 [1024, 2048], P('district', 'tile'), may hold values from 0.1 to 1
- child_wet: int32 [4, 1024, 2048], P(None, 'district', 'tile'), may hold values 0 or 1
- interior_state: float32 [3, 16384, 128], P(None, ('district', 'tile')), may hold values from -6 to 6
- interior_wet: int32 [4, 16384, 128], P(None, ('district', 'tile')), may hold values 0 or 1
- parent_anchor: int32 [16, 16, 2], P('district'), may hold values from 0 to 2044, as said below
- open_row: int32 [16384], P(('district', 'tile')), may hold values from 0 to 63
- open_col: int32 [16384], P(('district', 'tile')), may hold values from 0 to 96
- open_owner: int32 [16384, 1], P(('district', 'tile')), may hold values from 0 to 15; in each aligned block of 64 rows (0 to 63, 64 to 127, ...) at most 8 rows name the same one
- open_valid: int32 [16384], P(('district', 'tile')), may hold values 0 or 1
- open_conduct: float32 [16384], P(('district', 'tile')), may hold values from 0.1 to 0.5
- door_rows: int32 [256, 128], P(('district', 'tile')), may hold values from 0 to 63
Outputs:
- parent_final: float32 [3, 256, 2048], P(None, 'district', 'tile')
- child_final: float32 [3, 1024, 2048], P(None, 'district', 'tile')
- interior_final: float32 [3, 16384, 128], P(None, ('district', 'tile'))
The draws below stay inside these ranges and needn't reach their ends.
Inputs may be any that keep to these rules, and one draw needn't show every extreme that they name: `open_owner`: tile indices within the opening's own district group; among the rows of one device no owner is named by more than 8 rows, padded ones included. `parent_anchor`: entry 0 is the same for all tiles of a district and leaves room for 2 rows within the district's 16 parent rows; entry 1 rises by 4 from one tile to the next and every window lies within the parent grid's columns; district 0's windows start at column 0 and the last district's end at the grid's last column.
All inputs are finite; a program needn't handle non-finite values. No bound on the sum of `child_wet` or of `interior_wet` or of `open_valid` on one device may be relied on, other than what follows from the above.
Results may differ from the reference program's by a relative error of at most 0.0003.
Values sent between devices are 32-bit elements; how exact they have to be, the bound alone decides.
No kernel may reach another device: no remote copies, remote signals or barrier semaphores. Data moves between devices by JAX's collectives and lax.ppermute only.
A program may use at most 64 MiB of HBM per device.

```python
import math
import jax
import jax.numpy as jnp
import numpy as np
from jax import lax

PXD = 16
CX = 64
CY = 128
IX = 64
IY = 128
R = 32
STEPS = 4
CAP = 8
OPEN_DEV = 64
SEG = 32
WX = 2
WY = 4
PX = 256
PY = 2048
CXG = 1024
CYG = 2048
IXG = 16384
OPEN_ALL = 16384
N_DISTRICT = 16
N_TILE = 16
DEVICES = 256


def draw_parent_anchor(key, part):
    row_key = jax.random.fold_in(key, 11)
    col_key = jax.random.fold_in(key, 12)
    row_start = jax.random.randint(row_key, (N_DISTRICT, 1), 0, PXD - WX + 1)
    col_start = jax.random.randint(col_key, (N_DISTRICT, 1), 0, PY - N_TILE * WY + 1)
    district_ids = jnp.arange(N_DISTRICT, dtype=jnp.int32)[:, None]
    col_start = jnp.where(district_ids == 0, 0, col_start)
    col_start = jnp.where(district_ids == N_DISTRICT - 1, PY - N_TILE * WY, col_start)
    col_span = col_start + WY * jnp.arange(N_TILE, dtype=jnp.int32)[None, :]
    row_span = jnp.broadcast_to(row_start, (N_DISTRICT, N_TILE))
    return jnp.stack([row_span, col_span], -1).astype(jnp.int32)


def plant(array, key, smallest, largest):
    longest = array.shape.index(max(array.shape))
    spots = []
    for shift in (0, 1):
        where = [jax.random.randint(jax.random.fold_in(key, axis), (), 0, length) for axis, length in enumerate(array.shape)]
        where[longest] = (where[longest] + shift) % array.shape[longest]
        spots.append(tuple(where))
    return array.at[spots[0]].set(smallest).at[spots[1]].set(largest)


def level_of(rng, shape, shards, smallest, top_value):
    gain, own = 1.0, jax.random.fold_in(rng, 6)
    for position, shards_of in shards:
        steps = jnp.exp(jax.random.uniform(jax.random.fold_in(own, position), (shards_of,), jnp.float32, smallest / len(shards), top_value / len(shards)))
        gain = gain * jnp.repeat(steps, shape[position] // shards_of).reshape([-1 if axis == position else 1 for axis in range(len(shape))])
    return gain


def assign_block(own_key, own, number, rows, number_of, top, most, lean):
    order = jax.random.permutation(own_key, number_of)
    crowded, ordinary = portions_of(number_of, rows * top, most, lean, True), portions_of(number_of, rows * top, most, lean, False)
    places = jnp.arange(number_of)

    def named(lengths, offset_by):
        used = int((lengths > 0).sum())
        fixed = max(1, used // 4)
        moved = fixed + (places - fixed + offset_by * (used - fixed)) % max(1, number_of - fixed)
        return jnp.zeros((number_of,), jnp.int32).at[order[jnp.where(places < fixed, places, moved)]].set(jnp.asarray(lengths, jnp.int32))

    lengths = jnp.where(number % 4 == 0, named(crowded, number // 4), named(ordinary, number - number // 4 - 1))
    mixed = jax.random.permutation(jax.random.fold_in(own, 3), number_of)
    source_of, receiver = mixed[0:number_of // 2 * 2:2], mixed[1:number_of // 2 * 2:2]
    room = jnp.minimum(lengths[source_of] - 1, most - lengths[receiver]) // 2
    room = jnp.where((source_of == order[0]) | (receiver == order[0]) | (lengths[receiver] == 0), 0, jnp.maximum(room, 0))
    moved = jax.random.randint(jax.random.fold_in(own, 4), (number_of // 2,), 0, 1 << 20) % (room + 1)
    lengths = lengths.at[source_of].add(-moved).at[receiver].add(moved)
    labels = jnp.searchsorted(jnp.cumsum(lengths), jnp.arange(rows * top), side="right").astype(jnp.int32)
    table = labels.reshape(top, rows).T
    table = table[jax.random.permutation(jax.random.fold_in(own, 1), rows)]
    offset_by = jax.random.randint(jax.random.fold_in(own, 2), (rows, 1), 0, top)
    return jnp.take_along_axis(table, (jnp.arange(top)[None, :] + offset_by) % top, axis=1)


def portions_of(count, total, limit, skew, full):
    portions = [(1 << 20) // math.isqrt(rank ** skew) + 1 for rank in range(1, count + 1)]
    largest = limit if full else min(limit, max(-(-total // count), total * portions[0] // sum(portions)))
    least = 1 if total - largest >= count - 1 else 0
    holding, surplus = [largest] + [least] * (count - 1), total - largest - least * (count - 1)
    while surplus > 0:
        candidates = [i for i in range(1, count) if holding[i] < largest] or [i for i in range(1, count) if holding[i] < limit]
        pool, budget = sum([portions[i] for i in candidates]), surplus
        for i in candidates:
            more = min(limit - holding[i], max(1, budget * portions[i] // pool), surplus)
            holding[i] = holding[i] + more
            surplus = surplus - more
    return np.array(holding)


def noise(own_key, dims, spread, limit, pieces=(), kind=jnp.bfloat16):
    array = spread * jax.random.normal(own_key, dims, jnp.float32)
    if pieces:
        array = array * level_of(own_key, dims, pieces, -0.22, 0.18)
    return jnp.clip(array, -limit, limit).astype(kind)


def setup_inputs(seed: int = 0) -> dict:
    seeds = jax.random.split(jax.random.key(seed), 15)
    parent_state = noise(seeds[0], (3, PX, PY), 1.0, 6.0, ((1, 16), (2, 16)), jnp.float32)
    parent_depth = jnp.clip(jnp.exp(math.log(1.0) - 1.3862944 * jax.random.uniform(seeds[1], (PX, PY), jnp.float32) ** level_of(seeds[1], (PX, PY), ((0, 16), (1, 16)), -0.2, 0.2)), 0.25, 1.0)
    child_state = noise(seeds[2], (3, CXG, CYG), 1.0, 6.0, ((1, 16), (2, 16)), jnp.float32)
    child_depth = jnp.clip(jnp.exp(math.log(1.0) - 2.3025851 * jax.random.uniform(seeds[3], (CXG, CYG), jnp.float32) ** level_of(seeds[3], (CXG, CYG), ((0, 16), (1, 16)), -0.2, 0.2)), 0.1, 1.0)
    child_wet = plant((jax.random.randint(seeds[4], (STEPS, CXG, CYG), 0, 10) < 9).astype(jnp.int32), jax.random.fold_in(seeds[4], 1), 0, 1)
    interior_state = noise(seeds[5], (3, IXG, IY), 1.0, 6.0, ((1, 256),), jnp.float32)
    interior_wet = plant((jax.random.randint(seeds[6], (STEPS, IXG, IY), 0, 5) < 4).astype(jnp.int32), jax.random.fold_in(seeds[6], 1), 0, 1)
    parent_anchor = draw_parent_anchor(jax.random.fold_in(seeds[14], 71), 0)
    open_row = plant(jax.random.randint(seeds[8], (OPEN_ALL,), 0, CX), jax.random.fold_in(seeds[8], 1), 0, CX - 1).astype(jnp.int32)
    open_col = plant(jax.random.randint(seeds[9], (OPEN_ALL,), 0, CY - SEG + 1), jax.random.fold_in(seeds[9], 1), 0, CY - SEG).astype(jnp.int32)
    open_owner_keys = jax.random.split(jax.random.fold_in(seeds[10], 1), OPEN_ALL // OPEN_DEV)
    open_owner_turns = jax.random.permutation(jax.random.fold_in(seeds[10], 3), OPEN_ALL // OPEN_DEV)
    open_owner = jax.vmap(lambda own, number: assign_block(jax.random.fold_in(seeds[10], 2), own, number, OPEN_DEV, N_TILE, 1, CAP, 2))(open_owner_keys, open_owner_turns).reshape((OPEN_ALL, 1))
    open_valid = plant((jax.random.randint(seeds[11], (OPEN_ALL,), 0, 4) < 3).astype(jnp.int32), jax.random.fold_in(seeds[11], 1), 0, 1)
    open_conduct = jnp.clip(jnp.exp(math.log(0.5) - 1.609438 * jax.random.uniform(seeds[12], (OPEN_ALL,), jnp.float32) ** level_of(seeds[12], (OPEN_ALL,), ((0, 256),), -0.2, 0.2)), 0.1, 0.5)
    door_rows = plant(jax.random.randint(seeds[13], (DEVICES, N_TILE * CAP), 0, IX), jax.random.fold_in(seeds[13], 1), 0, IX - 1).astype(jnp.int32)
    return dict(parent_state=parent_state, parent_depth=parent_depth, child_state=child_state, child_depth=child_depth, child_wet=child_wet, interior_state=interior_state, interior_wet=interior_wet, parent_anchor=parent_anchor, open_row=open_row, open_col=open_col, open_owner=open_owner, open_valid=open_valid, open_conduct=open_conduct, door_rows=door_rows)


courant = 0.3
nudging = 0.25
area_ratio = 0.0625


def advance(padded, wet_cells):
    surface = padded[0]
    east_flow = padded[1]
    north_flow = padded[2]
    wet_depth = padded[3]
    new_east = east_flow[1:-1, 2:-2] - courant * (surface[2:, 2:-2] - surface[:-2, 2:-2])
    new_north = north_flow[2:-2, 1:-1] - courant * (surface[2:-2, 2:] - surface[2:-2, :-2])
    flux_east = wet_depth[1:-1, 2:-2] * new_east
    flux_north = wet_depth[2:-2, 1:-1] * new_north
    new_surface = surface[2:-2, 2:-2] - courant * (flux_east[2:] - flux_east[:-2] + flux_north[:, 2:] - flux_north[:, :-2])
    return new_surface, wet_cells * new_east[1:-1], wet_cells * new_north[:, 1:-1]


def stacked(state, wet_depth):
    return jnp.pad(jnp.concatenate([state, wet_depth[None]], 0), ((0, 0), (2, 2), (2, 2)))


def room_step(state, wet_cells):
    return jnp.stack(advance(stacked(state, wet_cells), wet_cells))


def ranks(owners, tile_count):
    matches = (owners[:, None] == jnp.arange(tile_count, dtype=jnp.int32)[None, :]).astype(jnp.int32)
    return jnp.sum(jnp.cumsum(matches, 0) * matches, 1) - 1


def place_rows(values, owners, slot_of, tile_count):
    empty = jnp.zeros((tile_count, CAP) + values.shape[1:], values.dtype)
    return empty.at[owners, slot_of].set(values)


def opening_flow(street, weights, face_rows):
    inflow = weights[..., None] * (jnp.repeat(street, 4, axis=-1) - face_rows)
    grouped = inflow.reshape(inflow.shape[:-1] + (inflow.shape[-1] // 4, 4))
    return inflow, jnp.sum(grouped, -1) * area_ratio


def absorb(surface, room_rows, street, weights):
    face_rows = surface[room_rows].reshape(weights.shape + (IY,))
    inflow, flux_back = opening_flow(street, weights, face_rows)
    return surface.at[room_rows].add(inflow.reshape(-1, IY)), flux_back


def apply_return(flat_level, cell_ids, owners, slot_of, returned):
    return flat_level.at[cell_ids].add(-returned[owners, slot_of])


def swap_pairs(values):
    shaped = values.reshape((N_DISTRICT, N_TILE, N_TILE) + values.shape[2:])
    return jnp.swapaxes(shaped, 1, 2).reshape(values.shape)


def cut_district(surface, district, anchors):
    def cut_one(anchor):
        return lax.dynamic_slice(surface, (district * PXD + anchor[0], anchor[1]), (WX, WY))
    return jax.vmap(cut_one)(anchors)


def reference(parent_state, parent_depth, child_state, child_depth, child_wet, interior_state, interior_wet, parent_anchor, open_row, open_col, open_owner, open_valid, open_conduct, door_rows):
    device_count = N_DISTRICT * N_TILE
    parent_now = parent_state
    child_now = child_state
    rooms_now = interior_state.reshape(3, device_count, IX, IY).transpose(1, 0, 2, 3)
    rooms_wet = interior_wet.reshape(STEPS, device_count, IX, IY).astype(jnp.float32)
    owners = open_owner[:, 0].reshape(device_count, OPEN_DEV)
    slot_of = jax.vmap(lambda o: ranks(o, N_TILE))(owners)
    starts = (open_row * CY + open_col).reshape(device_count, OPEN_DEV)
    cell_ids = starts[:, :, None] + jnp.arange(SEG, dtype=jnp.int32)[None, None, :]
    open_weight = (open_conduct * open_valid.astype(jnp.float32)).reshape(device_count, OPEN_DEV)
    weights = jax.vmap(lambda v, o, s: place_rows(v, o, s, N_TILE))(open_weight, owners, slot_of)
    district_ids = jnp.arange(N_DISTRICT, dtype=jnp.int32)
    for section_index in range(STEPS):
        surface, east_flow, north_flow = advance(stacked(parent_now, parent_depth), 1.0)
        parent_now = jnp.stack([surface, east_flow, north_flow])
        windows = jax.vmap(cut_district, in_axes=(None, 0, 0))(surface, district_ids, parent_anchor)
        target = jnp.broadcast_to(windows[:, :, :, None, :, None], (N_DISTRICT, N_TILE, WX, R, WY, R))
        target = target.reshape(N_DISTRICT, N_TILE, CX, CY).transpose(0, 2, 1, 3).reshape(N_DISTRICT * CX, N_TILE * CY)
        wet_now = child_wet[section_index].astype(jnp.float32)
        surface, east_flow, north_flow = advance(stacked(child_now, child_depth * wet_now), wet_now)
        surface = surface + nudging * (target - surface)
        rooms_now = jax.vmap(room_step)(rooms_now, rooms_wet[section_index])
        flat_level = surface.reshape(N_DISTRICT, CX, N_TILE, CY).transpose(0, 2, 1, 3).reshape(device_count, CX * CY)
        samples = jax.vmap(lambda f, c: f[c])(flat_level, cell_ids)
        street = jax.vmap(lambda v, o, s: place_rows(v, o, s, N_TILE))(samples, owners, slot_of)
        surfaces, flux_back = jax.vmap(absorb)(rooms_now[:, 0], door_rows, swap_pairs(street), swap_pairs(weights))
        rooms_now = rooms_now.at[:, 0].set(surfaces)
        flat_level = jax.vmap(apply_return)(flat_level, cell_ids, owners, slot_of, swap_pairs(flux_back))
        surface = flat_level.reshape(N_DISTRICT, N_TILE, CX, CY).transpose(0, 2, 1, 3).reshape(N_DISTRICT * CX, N_TILE * CY)
        child_now = jnp.stack([surface, east_flow, north_flow])
    interior_final = rooms_now.transpose(1, 0, 2, 3).reshape(3, device_count * IX, IY)
    return parent_now, child_now, interior_final
```

```python
import jax
import jax.numpy as jnp
from jax import lax
from jax.experimental import pallas as pl
from jax.experimental.pallas import tpu as pltpu
from jax.sharding import PartitionSpec as P

f32 = jnp.float32
bf16 = jnp.bfloat16
i32 = jnp.int32

CX = 64
PX = 16
LANES = 128
R = 32
STEPS = 4
CAP = 8
TILES = 16
SLOTS = TILES * CAP

courant = 0.3
nudging = 0.25
area_ratio = 0.0625

L_ROOM = 32
L_NEAR = 64
L_FIX = 68
L_PCOL = 72
L_WIN = 80
L_CCOL = 96


def lane(shape):
    return lax.broadcasted_iota(i32, shape, 1)


def sub(shape):
    return lax.broadcasted_iota(i32, shape, 0)


def roll(cells, by):
    return pltpu.roll(cells, by % LANES, 1)


def along(cells, index):
    return jnp.take_along_axis(cells, index, axis=1, mode="promise_in_bounds")


def halves(cells):
    high = cells.astype(bf16)
    low = (cells - high.astype(f32)).astype(bf16)
    return jnp.concatenate([high, low], 0)


def pick(selector, cells):
    return jnp.dot(selector, halves(cells), preferred_element_type=f32)


def pack4(packed, cells, at):
    at_lane = lane(packed.shape)
    for g in range(cells.shape[0] // 8):
        first = at + 4 * g
        moved = roll(cells[8 * g : 8 * g + 8], first + 2)
        packed = jnp.where((at_lane >= first) & (at_lane < first + 4), moved, packed)
    return packed


def pack2(packed, cells, at):
    at_lane = lane(packed.shape)
    for g in range(cells.shape[0] // 8):
        first = at + 2 * g
        moved = roll(cells[8 * g : 8 * g + 8], first + 1)
        packed = jnp.where((at_lane >= first) & (at_lane < first + 2), moved, packed)
    return packed


def unpack4(left, right, at, groups):
    chosen = jnp.where(lane(left.shape) % 4 >= 2, right, left)
    return jnp.concatenate([roll(chosen, -(at + 4 * g + 2)) for g in range(groups)], 0)


def unpack2(left, right, at, groups):
    chosen = jnp.where(lane(left.shape) % 2 == 1, right, left)
    return jnp.concatenate([roll(chosen, -(at + 2 * g + 1)) for g in range(groups)], 0)


def advance(eta_x, u_x, v, v_h, eta_h, q, q_up, q_dn, q_h, flux_x, rows):
    top, end = 8, 8 + rows
    at_lane = lane((rows, LANES))
    first, last = at_lane == 0, at_lane == LANES - 1
    eta = eta_x[top:end]
    u_new = u_x[top:end] - courant * (eta_x[top + 1 : end + 1] - eta_x[top - 1 : end - 1])
    u_up = u_x[top - 1 : top] - courant * (eta_x[top : top + 1] - eta_x[top - 2 : top - 1])
    u_dn = u_x[end : end + 1] - courant * (eta_x[end + 1 : end + 2] - eta_x[end - 1 : end])
    after = roll(jnp.where(first, eta_h, eta), -1)
    before = roll(jnp.where(last, eta_h, eta), 1)
    v_new = v - courant * (after - before)
    after = roll(jnp.where(first, eta, eta_h), -1)
    before = roll(jnp.where(last, eta, eta_h), 1)
    v_edge = v_h - courant * (after - before)
    flux_x[top:end] = q * u_new
    flux_x[top - 1 : top] = q_up * u_up
    flux_x[end : end + 1] = q_dn * u_dn
    flux = q * v_new
    flux_h = q_h * v_edge
    after = roll(jnp.where(first, flux_h, flux), -1)
    before = roll(jnp.where(last, flux_h, flux), 1)
    eta_new = eta - courant * (
        flux_x[top + 1 : end + 1] - flux_x[top - 1 : end - 1] + after - before
    )
    return eta_new, u_new, u_up, u_dn, v_new, v_edge


def wet_of(q):
    return jnp.where(q > 0, 1.0, 0.0).astype(f32)


def room_advance(eta, u, v, wet, eta_x, flux_x):
    at_lane = lane((CX, LANES))
    first, last = at_lane == 0, at_lane == LANES - 1
    blank = jnp.zeros((8, LANES), f32)
    for ref in (eta_x, flux_x):
        ref[0:8] = blank
        ref[8 + CX : 16 + CX] = blank
    eta_x[8 : 8 + CX] = eta
    u_new = u - courant * (eta_x[9 : 9 + CX] - eta_x[7 : 7 + CX])
    v_new = v - courant * (
        jnp.where(last, 0.0, roll(eta, -1)) - jnp.where(first, 0.0, roll(eta, 1))
    )
    flux_x[8 : 8 + CX] = wet * u_new
    flux = wet * v_new
    eta_new = eta - courant * (
        flux_x[9 : 9 + CX]
        - flux_x[7 : 7 + CX]
        + jnp.where(last, 0.0, roll(flux, -1))
        - jnp.where(first, 0.0, roll(flux, 1))
    )
    return eta_new, wet * u_new, wet * v_new


def room_reply(eta, door2, fixed):
    sums = eta + roll(eta, -1)
    sums = sums + roll(sums, -2)
    at_lane = lane((CX, LANES))
    sums = along(sums, (4 * (at_lane - L_ROOM)) & (LANES - 1))
    both = pick(door2, jnp.concatenate([eta, sums], 1))
    rows, sums = both[:, :LANES], both[:, LANES:]
    ahead = roll(jnp.concatenate([sums[8:], sums[:8]], 0), L_NEAR - L_ROOM)
    behind = roll(jnp.concatenate([sums[-8:], sums[:-8]], 0), L_NEAR + 2 - (L_ROOM + 30))
    at_lane = lane(sums.shape)
    reply = jnp.where(
        at_lane < L_NEAR,
        sums,
        jnp.where(at_lane < L_NEAR + 2, ahead, jnp.where(at_lane < L_FIX, behind, fixed)),
    )
    return rows, reply


def slots_of(side):
    shape = (SLOTS, LANES)
    held = sub(shape).astype(f32) == side[8:9]

    def take(values):
        return jnp.sum(jnp.where(held, values, 0.0), axis=1, keepdims=True)

    row = take(side[9:10] + 1.0) - 1.0
    return row.astype(i32), take(side[10:11]).astype(i32), take(side[11:12])


def edges_kernel(
    parent, parent_depth, child, child_depth, child_wet, row, col, owner, owner_t, valid, conduct, up, dn, side
):
    up[...] = jnp.zeros((16, LANES), f32)
    dn[...] = jnp.zeros((16, LANES), f32)
    side[...] = jnp.zeros((16, LANES), f32)
    eta = child[0]
    packed = pack4(jnp.zeros((8, LANES), f32), eta, 0)
    packed = pack2(packed, child[2], 32)
    up[0:2] = eta[0:2]
    dn[0:2] = eta[CX - 2 : CX]
    up[2:3] = child[1, 0:1]
    dn[2:3] = child[1, CX - 1 : CX]
    for s in range(STEPS):
        q = child_depth[...] * child_wet[s].astype(f32)
        up[3 + s : 4 + s] = q[0:1]
        dn[3 + s : 4 + s] = q[CX - 1 : CX]
        packed = pack2(packed, q, 48 + 16 * s)
    eta = parent[0]
    up[7:9] = eta[0:2]
    dn[7:9] = eta[PX - 2 : PX]
    up[9:10] = parent[1, 0:1]
    dn[9:10] = parent[1, PX - 1 : PX]
    up[10:11] = parent_depth[0:1]
    dn[10:11] = parent_depth[PX - 1 : PX]
    packed = pack4(packed, eta, 112)
    packed = pack2(packed, parent[2], 120)
    packed = pack2(packed, parent_depth[...], 124)
    side[0:8] = packed
    count = owner.shape[1]
    earlier = (owner_t[...] == owner[...]) & (sub((count, count)) < lane((count, count)))
    rank = jnp.sum(jnp.where(earlier, 1.0, 0.0), axis=0, keepdims=True)
    side[8:9] = jnp.full((1, LANES), -1.0, f32)
    side[8:9, 0:count] = owner[...].astype(f32) * CAP + rank
    side[9:10, 0:count] = row[...].astype(f32)
    side[10:11, 0:count] = col[...].astype(f32)
    side[11:12, 0:count] = conduct[...] * valid[...].astype(f32)


def setup_kernel(
    side, door, room, room_wet, row2, row_t2, index_s, index_a, gain, lower, fixed, door2, door_t2, room_new, face, reply, eta_x, flux_x
):
    shape = (SLOTS, LANES)
    at_lane = lane(shape)
    row, col, weight = slots_of(side[...])
    chosen = jnp.where(at_lane == row, 1.0, 0.0)
    row2[...] = (chosen + roll(chosen, CX)).astype(bf16)
    turned = jnp.transpose(chosen)[0:CX].astype(bf16)
    row_t2[...] = jnp.concatenate([turned, turned], 1)
    index_s[...] = (at_lane + col) & (LANES - 1)
    index_a[...] = (at_lane - col + L_ROOM) & (LANES - 1)
    inside = (at_lane >= col) & (at_lane < col + R)
    gain[...] = jnp.where(inside, area_ratio * weight, 0.0)
    half = jnp.where(row >= R, 1.0, 0.0)
    lower[...] = jnp.broadcast_to(half, shape)
    fixed_now = jnp.where(
        at_lane == L_FIX,
        weight,
        jnp.where(at_lane == L_FIX + 1, col.astype(f32), jnp.where(at_lane == L_FIX + 2, half, 0.0)),
    )
    fixed[...] = fixed_now
    chosen_t = jnp.where(sub(shape) == door[...], 1.0, 0.0)
    turned = chosen_t[0:CX].astype(bf16)
    door_t2[...] = jnp.concatenate([turned, turned], 1)
    chosen = jnp.transpose(chosen_t)
    both = (chosen + roll(chosen, CX)).astype(bf16)
    door2[...] = both
    eta, u, v = room_advance(room[0], room[1], room[2], room_wet[0].astype(f32), eta_x, flux_x)
    room_new[0] = eta
    room_new[1] = u
    room_new[2] = v
    face[...], reply[...] = room_reply(eta, both, fixed_now)


def near_kernel(left, right, row2, row_t2, index, gain):
    shape = (SLOTS, LANES)
    at_lane = lane(shape)
    turned = []
    for part, side in enumerate((right, left)):
        rows = slice(part * SLOTS, (part + 1) * SLOTS)
        row, col, weight = slots_of(side[...])
        chosen = jnp.where(at_lane == row, 1.0, 0.0)
        row2[rows] = (chosen + roll(chosen, CX)).astype(bf16)
        turned.append(jnp.transpose(chosen)[0:CX].astype(bf16))
        if part == 0:
            touched = (at_lane < 2) & (at_lane >= col)
            index[rows] = (at_lane - col + L_NEAR) & (LANES - 1)
        else:
            touched = (at_lane >= LANES - 2) & (at_lane < col + R)
            index[rows] = (at_lane - col + (L_NEAR + 2 - 30)) & (LANES - 1)
        gain[rows] = jnp.where(touched, area_ratio * weight, 0.0)
    row_t2[...] = jnp.concatenate(turned + turned, 1)


def send_kernel(step, *refs):
    if step == 0:
        (
            scal, parent, parent_depth, child, child_depth, child_wet, above0, below0, left0, right0, reply, row2, index_s,
            eta_o, u_o, v_o, vh_o, peta_o, pu_o, pv_o, pvh_o, street_o, out, eta_x, flux_x, u_x, peta_x, pflux_x, pu_x,
        ) = refs
        u_x[8 : 8 + CX] = child[1]
        u_x[7:8] = above0[2:3]
        u_x[8 + CX : 9 + CX] = below0[2:3]
        pu_x[8 : 8 + PX] = parent[1]
        pu_x[7:8] = above0[9:10]
        pu_x[8 + PX : 9 + PX] = below0[9:10]
        eta_x[8 : 8 + CX] = child[0]
        peta_x[8 : 8 + PX] = parent[0]
        eta_x[6:8] = above0[0:2]
        eta_x[8 + CX : 10 + CX] = below0[0:2]
        peta_x[6:8] = above0[7:9]
        peta_x[8 + PX : 10 + PX] = below0[7:9]
        left, right = left0[0:8], right0[0:8]
        v, v_h = child[2], unpack2(left, right, 32, 8)
        eta_h = unpack4(left, right, 0, 8)
        pv, pv_h = parent[2], unpack2(left, right, 120, 2)
        peta_h = unpack4(left, right, 112, 2)
    else:
        (
            scal, parent_depth, child_depth, child_wet, above0, below0, left0, right0, reply, row2, index_s,
            above, below, eta_i, u_x, v_i, vh_i, etah_i, peta_i, pu_x, pv_i, pvh_i, petah_i,
            eta_o, u_o, v_o, vh_o, peta_o, pu_o, pv_o, pvh_o, street_o, out, eta_x, flux_x, peta_x, pflux_x,
        ) = refs
        eta_x[8 : 8 + CX] = eta_i[...]
        peta_x[8 : 8 + PX] = peta_i[...]
        eta_x[6:8] = above[0:2]
        eta_x[8 + CX : 10 + CX] = below[0:2]
        peta_x[6:8] = above[2:4]
        peta_x[8 + PX : 10 + PX] = below[2:4]
        left, right = left0[0:8], right0[0:8]
        v, v_h, eta_h = v_i[...], vh_i[...], etah_i[...]
        pv, pv_h, peta_h = pv_i[...], pvh_i[...], petah_i[...]
    wet = child_wet[step].astype(f32)
    q = child_depth[...] * wet
    q_up, q_dn = above0[3 + step : 4 + step], below0[3 + step : 4 + step]
    q_h = unpack2(left, right, 48 + 16 * step, 8)
    eta, u, u_up, u_dn, v, v_h = advance(eta_x, u_x, v, v_h, eta_h, q, q_up, q_dn, q_h, flux_x, CX)
    street = pick(row2[...], eta)
    peta, pu, pu_up, pu_dn, pv, pv_h = advance(
        peta_x, pu_x, pv, pv_h, peta_h, parent_depth[...], above0[10:11], below0[10:11], unpack2(left, right, 124, 2), pflux_x, PX
    )
    eta_o[...] = eta
    u_o[8 : 8 + CX] = wet * u
    u_o[7:8] = wet_of(q_up) * u_up
    u_o[8 + CX : 9 + CX] = wet_of(q_dn) * u_dn
    v_o[...] = wet * v
    vh_o[...] = wet_of(q_h) * v_h
    peta_o[...] = peta
    pu_o[8 : 8 + PX] = pu
    pu_o[7:8] = pu_up
    pu_o[8 + PX : 9 + PX] = pu_dn
    pv_o[...] = pv
    pvh_o[...] = pv_h
    street_o[...] = street
    tile, first_row, first_col = scal[0], scal[1], scal[2]
    shape = (8, LANES)
    at_lane = lane(shape)
    common = pack4(jnp.zeros(shape, f32), eta, L_CCOL)
    common = pack4(common, peta, L_PCOL)
    line0 = peta_o[pl.ds(first_row, 1)]
    line1 = peta_o[pl.ds(first_row + 1, 1)]
    lines = jnp.where(sub(shape) < 4, line0, line1)
    index = first_col - LANES * tile + 4 * (at_lane - L_WIN) + (sub(shape) & 3)
    window = along(lines, index & (LANES - 1))
    window = jnp.where((index >= 0) & (index < LANES), window, 0.0)
    common = jnp.where((at_lane >= L_WIN) & (at_lane < L_CCOL), window, common)
    street = along(street, index_s[...])
    for t in range(TILES):
        rows = slice(t * CAP, (t + 1) * CAP)
        out[rows] = jnp.where(at_lane < R, street[rows], jnp.where(at_lane < L_PCOL, reply[rows], common))


def windows_sum(inbox):
    parts = [inbox[8 * t : 8 * t + 8] for t in range(TILES)]
    while len(parts) > 1:
        parts = [parts[i] + parts[i + 1] for i in range(0, len(parts), 2)]
    return parts[0]


def nudge(eta, target):
    return eta + nudging * (target - eta)


def street_update(scal, inbox, eta, street, row_t2, index_a, gain, lower):
    shape = (8, LANES)
    windows = windows_sum(inbox)
    mine = along(windows, jnp.full(shape, L_WIN, i32) + scal[0])
    mine = jnp.where((sub(shape) & 3) == lane(shape) // R, mine, 0.0)
    target0 = jnp.sum(mine[0:4], axis=0, keepdims=True)
    target1 = jnp.sum(mine[4:8], axis=0, keepdims=True)
    eta = jnp.concatenate([nudge(eta[0:R], target0), nudge(eta[R:CX], target1)], 0)
    levels = nudge(street, jnp.where(lower > 0, target1, target0))
    flow = gain * (4.0 * levels - along(inbox, index_a))
    return eta - pick(row_t2, flow), windows


def room_flow(inbox, windows, face):
    shape = (SLOTS, LANES)
    at_lane = lane(shape)
    holder = jnp.where(at_lane == L_WIN + sub(shape) // CAP, 1.0, 0.0).astype(bf16)
    high = windows.astype(bf16)
    low = (windows - high.astype(f32)).astype(bf16)
    per_slot = lax.dot_general(
        jnp.concatenate([holder, holder], 1),
        jnp.concatenate([jnp.concatenate([high, low], 1), jnp.zeros((LANES - 8, 2 * LANES), bf16)], 0),
        (((1,), (1,)), ((), ())),
        preferred_element_type=f32,
    )
    weight = inbox[:, L_FIX : L_FIX + 1]
    col = inbox[:, L_FIX + 1 : L_FIX + 2].astype(i32)
    half = inbox[:, L_FIX + 2 : L_FIX + 3].astype(i32)
    cell = at_lane // 4
    target = along(per_slot, 4 * half + ((col + cell) // R & 3))
    levels = nudge(along(inbox, cell), target)
    return weight * (levels - face)


def street_kernel(scal, inbox, eta, street, row_t2, index_a, gain, lower, peta, eta_o, up, dn, windows_o):
    eta, windows_o[...] = street_update(
        scal, inbox[...], eta[...], street[...], row_t2[...], index_a[...], gain[...], lower[...]
    )
    eta_o[...] = eta
    blank = jnp.zeros((4, LANES), f32)
    up[0:2] = eta[0:2]
    up[2:4] = peta[0:2]
    up[4:8] = blank
    dn[0:2] = eta[CX - 2 : CX]
    dn[2:4] = peta[PX - 2 : PX]
    dn[4:8] = blank


def room_kernel(
    step, scal, inbox, windows, room, room_wet, face, door2, door_t2, fixed, near2, near_t2, near_index, near_gain,
    room_new, face_o, reply, etah_o, petah_o, eta_x, flux_x,
):
    received = inbox[...]
    flow = room_flow(received, windows[...], face[...])
    eta = room[0] + pick(door_t2[...], flow)
    eta, u, v = room_advance(eta, room[1], room[2], room_wet[step].astype(f32), eta_x, flux_x)
    room_new[0] = eta
    room_new[1] = u
    room_new[2] = v
    face_o[...], reply[...] = room_reply(eta, door2[...], fixed[...])
    tile = scal[0]
    left = inbox[pl.ds(pl.multiple_of(8 * lax.rem(tile + TILES - 1, TILES), 8), 8)]
    right = inbox[pl.ds(pl.multiple_of(8 * lax.rem(tile + 1, TILES), 8), 8)]
    at_lane = lane((8, LANES))

    def kept(cells):
        return jnp.where(jnp.where(lane(cells.shape) < R, TILES - 1 - tile, tile) > 0, cells, 0.0)

    petah_o[...] = kept(unpack4(left, right, L_PCOL, 2))
    eta_h = unpack4(left, right, L_CCOL, 8)
    spread = along(windows[...], L_WIN + ((jnp.where(at_lane < R, tile + 1, tile - 1)) & (TILES - 1)))
    target0 = jnp.where(at_lane < R, spread[0:1], spread[3:4])
    target1 = jnp.where(at_lane < R, spread[4:5], spread[7:8])
    eta_h = nudge(eta_h, jnp.concatenate([target0] * 4 + [target1] * 4, 0))
    levels = pick(near2[...], eta_h)
    sums = along(jnp.concatenate([received, received], 0), near_index[...])
    eta_h = eta_h - pick(near_t2[...], near_gain[...] * (4.0 * levels - sums))
    etah_o[...] = kept(eta_h)


def final_kernel(
    scal, inbox, eta, street, row_t2, index_a, gain, lower, u_x, v, peta, pu_x, pv, room, face, door_t2,
    parent_o, child_o, room_o,
):
    received = inbox[...]
    eta, windows = street_update(scal, received, eta[...], street[...], row_t2[...], index_a[...], gain[...], lower[...])
    child_o[0] = eta
    child_o[1] = u_x[8 : 8 + CX]
    child_o[2] = v[...]
    parent_o[0] = peta[...]
    parent_o[1] = pu_x[8 : 8 + PX]
    parent_o[2] = pv[...]
    room_o[0] = room[0] + pick(door_t2[...], room_flow(received, windows, face[...]))
    room_o[1] = room[1]
    room_o[2] = room[2]


def sds(*shape, dtype=f32):
    return jax.ShapeDtypeStruct(shape, dtype)


def call(name, kernel, outs, args, scalars=0, scratch=(), us=1):
    spec = pl.BlockSpec(memory_space=pltpu.VMEM)
    return pl.pallas_call(
        kernel,
        out_shape=outs,
        in_specs=[pl.BlockSpec(memory_space=pltpu.SMEM)] * scalars + [spec] * (len(args) - scalars),
        out_specs=jax.tree.map(lambda _: spec, outs),
        scratch_shapes=[pltpu.VMEM((rows, LANES), f32) for rows in scratch],
        compiler_params=pltpu.CompilerParams(vmem_limit_bytes=16 * 2**20),
        cost_estimate=pl.CostEstimate(flops=1000000 * us, bytes_accessed=1000000 * us, transcendentals=0),
        name=name,
    )(*args)


def shifts(up, dn, axis):
    count = lax.axis_size(axis)
    before = lax.ppermute(dn, axis, [(i, i + 1) for i in range(count - 1)])
    after = lax.ppermute(up, axis, [(i + 1, i) for i in range(count - 1)])
    return before, after


def body(
    parent_state,
    parent_depth,
    child_state,
    child_depth,
    child_wet,
    interior_state,
    interior_wet,
    parent_anchor,
    open_row,
    open_col,
    open_owner,
    open_valid,
    open_conduct,
    door_rows,
):
    block, tall = sds(CX, LANES), sds(CX + 16, LANES)
    pblock, ptall = sds(PX, LANES), sds(PX + 16, LANES)
    grid, tile8, tile16 = sds(SLOTS, LANES), sds(8, LANES), sds(16, LANES)
    rooms = sds(3, CX, LANES)
    my_tile = lax.axis_index("tile").astype(i32)
    scal = jnp.stack([my_tile, parent_anchor[0, 0, 0], parent_anchor[0, 0, 1], my_tile])

    def flat(values):
        return values.reshape(1, -1)

    up, dn, side = call(
        "edges",
        edges_kernel,
        [tile16] * 3,
        [
            parent_state, parent_depth, child_state, child_depth, child_wet, flat(open_row), flat(open_col),
            flat(open_owner), open_owner, flat(open_valid), flat(open_conduct),
        ],
    )
    above0, below0 = shifts(up, dn, "district")
    left0, right0 = shifts(side, side, "tile")
    row2, row_t2, index_s, index_a, gain, lower, fixed, door2, door_t2, room, face, reply = call(
        "setup",
        setup_kernel,
        [
            sds(SLOTS, LANES, dtype=bf16), sds(CX, 2 * SLOTS, dtype=bf16), sds(SLOTS, LANES, dtype=i32),
            sds(SLOTS, LANES, dtype=i32), grid, grid, grid, sds(SLOTS, LANES, dtype=bf16),
            sds(CX, 2 * SLOTS, dtype=bf16), rooms, grid, grid,
        ],
        [side, door_rows, interior_state, interior_wet],
        scratch=(CX + 16, CX + 16),
        us=4,
    )
    near = call(
        "near",
        near_kernel,
        [
            sds(2 * SLOTS, LANES, dtype=bf16), sds(CX, 4 * SLOTS, dtype=bf16), sds(2 * SLOTS, LANES, dtype=i32),
            sds(2 * SLOTS, LANES),
        ],
        [left0, right0],
        us=3,
    )
    outs = [block, tall, block, block, pblock, ptall, pblock, pblock, grid, grid]
    for step in range(STEPS):
        with_step = lambda *refs, step=step: send_kernel(step, *refs)
        if step == 0:
            args = [
                scal, parent_state, parent_depth, child_state, child_depth, child_wet, above0, below0, left0, right0,
                reply, row2, index_s,
            ]
            scratch = (CX + 16,) * 3 + (PX + 16,) * 3
        else:
            args = [
                scal, parent_depth, child_depth, child_wet, above0, below0, left0, right0, reply, row2, index_s,
                above, below, eta, u, v, v_h, eta_h, peta, pu, pv, pv_h, peta_h,
            ]
            scratch = (CX + 16,) * 2 + (PX + 16,) * 2
        eta, u, v, v_h, peta, pu, pv, pv_h, street, outbox = call(
            f"send{step}", with_step, outs, args, scalars=1, scratch=scratch
        )
        inbox = lax.all_to_all(outbox, "tile", split_axis=0, concat_axis=0, tiled=True)
        shared = [scal, inbox, eta, street, row_t2, index_a, gain, lower]
        if step == STEPS - 1:
            return tuple(
                call(
                    "final",
                    final_kernel,
                    [sds(3, PX, LANES), rooms, rooms],
                    shared + [u, v, peta, pu, pv, room, face, door_t2],
                    scalars=1,
                )
            )
        eta, up, dn, windows = call(
            f"street{step}", street_kernel, [block, tile8, tile8, tile8], shared + [peta], scalars=1
        )
        above, below = shifts(up, dn, "district")
        with_step = lambda *refs, step=step: room_kernel(step + 1, *refs)
        room, face, reply, eta_h, peta_h = call(
            f"room{step}",
            with_step,
            [rooms, grid, grid, block, pblock],
            [scal, inbox, windows, room, interior_wet, face, door2, door_t2, fixed, *near],
            scalars=1,
            scratch=(CX + 16, CX + 16),
            us=3,
        )


def solution(mesh):
    return jax.shard_map(
        body,
        mesh=mesh,
        in_specs=(
            P(None, "district", "tile"),
            P("district", "tile"),
            P(None, "district", "tile"),
            P("district", "tile"),
            P(None, "district", "tile"),
            P(None, ("district", "tile"), None),
            P(None, ("district", "tile"), None),
            P("district", None, None),
            P(("district", "tile")),
            P(("district", "tile")),
            P(("district", "tile"), None),
            P(("district", "tile")),
            P(("district", "tile")),
            P(("district", "tile"), None),
        ),
        out_specs=(
            P(None, "district", "tile"),
            P(None, "district", "tile"),
            P(None, ("district", "tile"), None),
        ),
        check_vma=False,
    )
```

```python
import jax
import jax.numpy as jnp
from jax import lax
from jax.experimental import pallas as pl
from jax.experimental.pallas import tpu as pltpu
from jax.sharding import PartitionSpec as P

f32 = jnp.float32
bf16 = jnp.bfloat16
i32 = jnp.int32

CX = 64
PX = 16
LANES = 128
R = 32
STEPS = 4
CAP = 8
TILES = 16
SLOTS = TILES * CAP

courant = 0.3
nudging = 0.25
area_ratio = 0.0625

L_ROOM = 32
L_NEAR = 64
L_FIX = 68
L_PCOL = 72
L_WIN = 80
L_CCOL = 96


def lane(shape):
    return lax.broadcasted_iota(i32, shape, 1)


def sub(shape):
    return lax.broadcasted_iota(i32, shape, 0)


def roll(cells, by):
    return pltpu.roll(cells, by % LANES, 1)


def along(cells, index):
    return jnp.take_along_axis(cells, index, axis=1, mode="promise_in_bounds")


def halves(cells):
    high = cells.astype(bf16)
    low = (cells - high.astype(f32)).astype(bf16)
    return jnp.concatenate([high, low], 0)


def pick(selector, cells):
    return jnp.dot(selector, halves(cells), preferred_element_type=f32)


def pack4(packed, cells, at):
    at_lane = lane(packed.shape)
    for g in range(cells.shape[0] // 8):
        first = at + 4 * g
        moved = roll(cells[8 * g : 8 * g + 8], first + 2)
        packed = jnp.where((at_lane >= first) & (at_lane < first + 4), moved, packed)
    return packed


def pack2(packed, cells, at):
    at_lane = lane(packed.shape)
    for g in range(cells.shape[0] // 8):
        first = at + 2 * g
        moved = roll(cells[8 * g : 8 * g + 8], first + 1)
        packed = jnp.where((at_lane >= first) & (at_lane < first + 2), moved, packed)
    return packed


def unpack4(left, right, at, groups):
    chosen = jnp.where(lane(left.shape) % 4 >= 2, right, left)
    return jnp.concatenate([roll(chosen, -(at + 4 * g + 2)) for g in range(groups)], 0)


def unpack2(left, right, at, groups):
    chosen = jnp.where(lane(left.shape) % 2 == 1, right, left)
    return jnp.concatenate([roll(chosen, -(at + 2 * g + 1)) for g in range(groups)], 0)


def advance(eta_x, u_x, v, v_h, eta_h, q, q_up, q_dn, q_h, flux_x, rows):
    top, end = 8, 8 + rows
    at_lane = lane((rows, LANES))
    first, last = at_lane == 0, at_lane == LANES - 1
    eta = eta_x[top:end]
    u_new = u_x[top:end] - courant * (eta_x[top + 1 : end + 1] - eta_x[top - 1 : end - 1])
    u_up = u_x[top - 1 : top] - courant * (eta_x[top : top + 1] - eta_x[top - 2 : top - 1])
    u_dn = u_x[end : end + 1] - courant * (eta_x[end + 1 : end + 2] - eta_x[end - 1 : end])
    after = roll(jnp.where(first, eta_h, eta), -1)
    before = roll(jnp.where(last, eta_h, eta), 1)
    v_new = v - courant * (after - before)
    after = roll(jnp.where(first, eta, eta_h), -1)
    before = roll(jnp.where(last, eta, eta_h), 1)
    v_edge = v_h - courant * (after - before)
    flux_x[top:end] = q * u_new
    flux_x[top - 1 : top] = q_up * u_up
    flux_x[end : end + 1] = q_dn * u_dn
    flux = q * v_new
    flux_h = q_h * v_edge
    after = roll(jnp.where(first, flux_h, flux), -1)
    before = roll(jnp.where(last, flux_h, flux), 1)
    eta_new = eta - courant * (
        flux_x[top + 1 : end + 1] - flux_x[top - 1 : end - 1] + after - before
    )
    return eta_new, u_new, u_up, u_dn, v_new, v_edge


def wet_of(q):
    return jnp.where(q > 0, 1.0, 0.0).astype(f32)


def room_advance(eta, u, v, wet, eta_x, flux_x):
    at_lane = lane((CX, LANES))
    first, last = at_lane == 0, at_lane == LANES - 1
    blank = jnp.zeros((8, LANES), f32)
    for ref in (eta_x, flux_x):
        ref[0:8] = blank
        ref[8 + CX : 16 + CX] = blank
    eta_x[8 : 8 + CX] = eta
    u_new = u - courant * (eta_x[9 : 9 + CX] - eta_x[7 : 7 + CX])
    v_new = v - courant * (
        jnp.where(last, 0.0, roll(eta, -1)) - jnp.where(first, 0.0, roll(eta, 1))
    )
    flux_x[8 : 8 + CX] = wet * u_new
    flux = wet * v_new
    eta_new = eta - courant * (
        flux_x[9 : 9 + CX]
        - flux_x[7 : 7 + CX]
        + jnp.where(last, 0.0, roll(flux, -1))
        - jnp.where(first, 0.0, roll(flux, 1))
    )
    return eta_new, wet * u_new, wet * v_new


def room_reply(eta, door2, fixed):
    sums = eta + roll(eta, -1)
    sums = sums + roll(sums, -2)
    at_lane = lane((CX, LANES))
    sums = along(sums, (4 * (at_lane - L_ROOM)) & (LANES - 1))
    both = pick(door2, jnp.concatenate([eta, sums], 1))
    rows, sums = both[:, :LANES], both[:, LANES:]
    ahead = roll(jnp.concatenate([sums[8:], sums[:8]], 0), L_NEAR - L_ROOM)
    behind = roll(jnp.concatenate([sums[-8:], sums[:-8]], 0), L_NEAR + 2 - (L_ROOM + 30))
    at_lane = lane(sums.shape)
    reply = jnp.where(
        at_lane < L_NEAR,
        sums,
        jnp.where(at_lane < L_NEAR + 2, ahead, jnp.where(at_lane < L_FIX, behind, fixed)),
    )
    return rows, reply


def slots_of(side):
    shape = (SLOTS, LANES)
    owner = jnp.broadcast_to(side[8:9], shape)
    earlier = (jnp.transpose(owner) == owner) & (sub(shape) < lane(shape))
    rank = jnp.sum(jnp.where(earlier, 1.0, 0.0), axis=0, keepdims=True)
    held = sub(shape).astype(f32) == jnp.where(side[8:9] >= 0, side[8:9] * CAP + rank, -1.0)

    def take(values):
        return jnp.sum(jnp.where(held, values, 0.0), axis=1, keepdims=True)

    row = take(side[9:10] + 1.0) - 1.0
    return row.astype(i32), take(side[10:11]).astype(i32), take(side[11:12])


def edges_kernel(
    parent_i, parent_depth_i, child_i, child_depth_i, child_wet_i, row_i, col_i, owner_i, valid_i, conduct_i, up, dn, side,
    parent, parent_depth, child, child_depth, child_wet, row, col, owner, valid, conduct, done,
):
    pairs = [
        (child_i, child), (child_depth_i, child_depth), (child_wet_i, child_wet), (parent_i, parent),
        (parent_depth_i, parent_depth), (row_i, row), (col_i, col), (owner_i, owner), (valid_i, valid), (conduct_i, conduct),
    ]
    copies = [pltpu.make_async_copy(src, dst, done.at[k]) for k, (src, dst) in enumerate(pairs)]
    for copy in copies:
        copy.start()
    up[...] = jnp.zeros((16, LANES), f32)
    dn[...] = jnp.zeros((16, LANES), f32)
    side[...] = jnp.zeros((16, LANES), f32)
    for copy in copies:
        copy.wait()
    eta = child[0]
    packed = pack4(jnp.zeros((8, LANES), f32), eta, 0)
    packed = pack2(packed, child[2], 32)
    up[0:2] = eta[0:2]
    dn[0:2] = eta[CX - 2 : CX]
    up[2:3] = child[1, 0:1]
    dn[2:3] = child[1, CX - 1 : CX]
    for s in range(STEPS):
        q = child_depth[...] * child_wet[s].astype(f32)
        up[3 + s : 4 + s] = q[0:1]
        dn[3 + s : 4 + s] = q[CX - 1 : CX]
        packed = pack2(packed, q, 48 + 16 * s)
    eta = parent[0]
    up[7:9] = eta[0:2]
    dn[7:9] = eta[PX - 2 : PX]
    up[9:10] = parent[1, 0:1]
    dn[9:10] = parent[1, PX - 1 : PX]
    up[10:11] = parent_depth[0:1]
    dn[10:11] = parent_depth[PX - 1 : PX]
    packed = pack4(packed, eta, 112)
    packed = pack2(packed, parent[2], 120)
    packed = pack2(packed, parent_depth[...], 124)
    side[0:8] = packed
    count = owner.shape[1]
    side[8:9] = jnp.full((1, LANES), -1.0, f32)
    side[8:9, 0:count] = owner[...].astype(f32)
    side[9:10, 0:count] = row[...].astype(f32)
    side[10:11, 0:count] = col[...].astype(f32)
    side[11:12, 0:count] = conduct[...] * valid[...].astype(f32)


def setup_kernel(
    side, door, room, room_wet, row2, row_t2, index_s, index_a, gain, lower, fixed, door2, door_t2, room_new, face, reply, eta_x, flux_x
):
    shape = (SLOTS, LANES)
    at_lane = lane(shape)
    row, col, weight = slots_of(side[...])
    chosen = jnp.where(at_lane == row, 1.0, 0.0)
    row2[...] = (chosen + roll(chosen, CX)).astype(bf16)
    turned = jnp.transpose(chosen)[0:CX].astype(bf16)
    row_t2[...] = jnp.concatenate([turned, turned], 1)
    index_s[...] = (at_lane + col) & (LANES - 1)
    index_a[...] = (at_lane - col + L_ROOM) & (LANES - 1)
    inside = (at_lane >= col) & (at_lane < col + R)
    gain[...] = jnp.where(inside, area_ratio * weight, 0.0)
    half = jnp.where(row >= R, 1.0, 0.0)
    lower[...] = jnp.broadcast_to(half, shape)
    fixed_now = jnp.where(
        at_lane == L_FIX,
        weight,
        jnp.where(at_lane == L_FIX + 1, col.astype(f32), jnp.where(at_lane == L_FIX + 2, half, 0.0)),
    )
    fixed[...] = fixed_now
    chosen_t = jnp.where(sub(shape) == door[...], 1.0, 0.0)
    turned = chosen_t[0:CX].astype(bf16)
    door_t2[...] = jnp.concatenate([turned, turned], 1)
    chosen = jnp.transpose(chosen_t)
    both = (chosen + roll(chosen, CX)).astype(bf16)
    door2[...] = both
    eta, u, v = room_advance(room[0], room[1], room[2], room_wet[0].astype(f32), eta_x, flux_x)
    room_new[0] = eta
    room_new[1] = u
    room_new[2] = v
    face[...], reply[...] = room_reply(eta, both, fixed_now)


def near_kernel(left, right, row2, row_t2, index, gain):
    shape = (SLOTS, LANES)
    at_lane = lane(shape)
    turned = []
    for part, side in enumerate((right, left)):
        rows = slice(part * SLOTS, (part + 1) * SLOTS)
        row, col, weight = slots_of(side[...])
        chosen = jnp.where(at_lane == row, 1.0, 0.0)
        row2[rows] = (chosen + roll(chosen, CX)).astype(bf16)
        turned.append(jnp.transpose(chosen)[0:CX].astype(bf16))
        if part == 0:
            touched = (at_lane < 2) & (at_lane >= col)
            index[rows] = (at_lane - col + L_NEAR) & (LANES - 1)
        else:
            touched = (at_lane >= LANES - 2) & (at_lane < col + R)
            index[rows] = (at_lane - col + (L_NEAR + 2 - 30)) & (LANES - 1)
        gain[rows] = jnp.where(touched, area_ratio * weight, 0.0)
    row_t2[...] = jnp.concatenate(turned + turned, 1)


def gate(there, cells):
    return jnp.where(there, cells, 0.0)


def send_kernel(step, *refs):
    scal = refs[0]
    has_left, has_right = scal[0] > 0, scal[0] < TILES - 1
    has_above, has_below = scal[3] > 0, scal[3] < scal[4] - 1
    if step == 0:
        (
            scal, parent, parent_depth, child, child_depth, child_wet, above0, below0, left0, right0, reply, row2, index_s,
            eta_o, u_o, v_o, vh_o, peta_o, pu_o, pv_o, pvh_o, street_o, out, eta_x, flux_x, u_x, peta_x, pflux_x, pu_x,
        ) = refs
        u_x[8 : 8 + CX] = child[1]
        u_x[7:8] = gate(has_above, above0[2:3])
        u_x[8 + CX : 9 + CX] = gate(has_below, below0[2:3])
        pu_x[8 : 8 + PX] = parent[1]
        pu_x[7:8] = gate(has_above, above0[9:10])
        pu_x[8 + PX : 9 + PX] = gate(has_below, below0[9:10])
        eta_x[8 : 8 + CX] = child[0]
        peta_x[8 : 8 + PX] = parent[0]
        eta_x[6:8] = gate(has_above, above0[0:2])
        eta_x[8 + CX : 10 + CX] = gate(has_below, below0[0:2])
        peta_x[6:8] = gate(has_above, above0[7:9])
        peta_x[8 + PX : 10 + PX] = gate(has_below, below0[7:9])
        left, right = gate(has_left, left0[0:8]), gate(has_right, right0[0:8])
        v, v_h = child[2], unpack2(left, right, 32, 8)
        eta_h = unpack4(left, right, 0, 8)
        pv, pv_h = parent[2], unpack2(left, right, 120, 2)
        peta_h = unpack4(left, right, 112, 2)
    else:
        (
            scal, parent_depth, child_depth, child_wet, above0, below0, left0, right0, reply, row2, index_s,
            above, below, eta_i, u_x, v_i, vh_i, etah_i, peta_i, pu_x, pv_i, pvh_i, petah_i,
            eta_o, u_o, v_o, vh_o, peta_o, pu_o, pv_o, pvh_o, street_o, out, eta_x, flux_x, peta_x, pflux_x,
        ) = refs
        eta_x[8 : 8 + CX] = eta_i[...]
        peta_x[8 : 8 + PX] = peta_i[...]
        eta_x[6:8] = gate(has_above, above[0:2])
        eta_x[8 + CX : 10 + CX] = gate(has_below, below[0:2])
        peta_x[6:8] = gate(has_above, above[2:4])
        peta_x[8 + PX : 10 + PX] = gate(has_below, below[2:4])
        left, right = gate(has_left, left0[0:8]), gate(has_right, right0[0:8])
        v, v_h, eta_h = v_i[...], vh_i[...], etah_i[...]
        pv, pv_h, peta_h = pv_i[...], pvh_i[...], petah_i[...]
    wet = child_wet[step].astype(f32)
    q = child_depth[...] * wet
    q_up = gate(has_above, above0[3 + step : 4 + step])
    q_dn = gate(has_below, below0[3 + step : 4 + step])
    pq_up, pq_dn = gate(has_above, above0[10:11]), gate(has_below, below0[10:11])
    q_h = unpack2(left, right, 48 + 16 * step, 8)
    eta, u, u_up, u_dn, v, v_h = advance(eta_x, u_x, v, v_h, eta_h, q, q_up, q_dn, q_h, flux_x, CX)
    street = pick(row2[...], eta)
    peta, pu, pu_up, pu_dn, pv, pv_h = advance(
        peta_x, pu_x, pv, pv_h, peta_h, parent_depth[...], pq_up, pq_dn, unpack2(left, right, 124, 2), pflux_x, PX
    )
    eta_o[...] = eta
    u_o[8 : 8 + CX] = wet * u
    u_o[7:8] = wet_of(q_up) * u_up
    u_o[8 + CX : 9 + CX] = wet_of(q_dn) * u_dn
    v_o[...] = wet * v
    vh_o[...] = wet_of(q_h) * v_h
    peta_o[...] = peta
    pu_o[8 : 8 + PX] = pu
    pu_o[7:8] = pu_up
    pu_o[8 + PX : 9 + PX] = pu_dn
    pv_o[...] = pv
    pvh_o[...] = pv_h
    street_o[...] = street
    tile, first_row, first_col = scal[0], scal[1], scal[2]
    shape = (8, LANES)
    at_lane = lane(shape)
    common = pack4(jnp.zeros(shape, f32), eta, L_CCOL)
    common = pack4(common, peta, L_PCOL)
    line0 = peta_o[pl.ds(first_row, 1)]
    line1 = peta_o[pl.ds(first_row + 1, 1)]
    lines = jnp.where(sub(shape) < 4, line0, line1)
    index = first_col - LANES * tile + 4 * (at_lane - L_WIN) + (sub(shape) & 3)
    window = along(lines, index & (LANES - 1))
    window = jnp.where((index >= 0) & (index < LANES), window, 0.0)
    common = jnp.where((at_lane >= L_WIN) & (at_lane < L_CCOL), window, common)
    street = along(street, index_s[...])
    for t in range(TILES):
        rows = slice(t * CAP, (t + 1) * CAP)
        out[rows] = jnp.where(at_lane < R, street[rows], jnp.where(at_lane < L_PCOL, reply[rows], common))


def windows_sum(inbox):
    parts = [inbox[8 * t : 8 * t + 8] for t in range(TILES)]
    while len(parts) > 1:
        parts = [parts[i] + parts[i + 1] for i in range(0, len(parts), 2)]
    return parts[0]


def nudge(eta, target):
    return eta + nudging * (target - eta)


def street_update(scal, inbox, eta, street, row_t2, index_a, gain, lower):
    shape = (8, LANES)
    windows = windows_sum(inbox)
    mine = along(windows, jnp.full(shape, L_WIN, i32) + scal[0])
    mine = jnp.where((sub(shape) & 3) == lane(shape) // R, mine, 0.0)
    target0 = jnp.sum(mine[0:4], axis=0, keepdims=True)
    target1 = jnp.sum(mine[4:8], axis=0, keepdims=True)
    eta = jnp.concatenate([nudge(eta[0:R], target0), nudge(eta[R:CX], target1)], 0)
    levels = nudge(street, jnp.where(lower > 0, target1, target0))
    flow = gain * (4.0 * levels - along(inbox, index_a))
    return eta - pick(row_t2, flow), windows


def room_flow(inbox, windows, face):
    shape = (SLOTS, LANES)
    at_lane = lane(shape)
    holder = jnp.where(at_lane == L_WIN + sub(shape) // CAP, 1.0, 0.0).astype(bf16)
    high = windows.astype(bf16)
    low = (windows - high.astype(f32)).astype(bf16)
    per_slot = lax.dot_general(
        jnp.concatenate([holder, holder], 1),
        jnp.concatenate([jnp.concatenate([high, low], 1), jnp.zeros((LANES - 8, 2 * LANES), bf16)], 0),
        (((1,), (1,)), ((), ())),
        preferred_element_type=f32,
    )
    weight = inbox[:, L_FIX : L_FIX + 1]
    col = inbox[:, L_FIX + 1 : L_FIX + 2].astype(i32)
    half = inbox[:, L_FIX + 2 : L_FIX + 3].astype(i32)
    cell = at_lane // 4
    target = along(per_slot, 4 * half + ((col + cell) // R & 3))
    levels = nudge(along(inbox, cell), target)
    return weight * (levels - face)


def street_kernel(scal, inbox, eta, street, row_t2, index_a, gain, lower, peta, eta_o, up, dn, windows_o):
    eta, windows_o[...] = street_update(
        scal, inbox[...], eta[...], street[...], row_t2[...], index_a[...], gain[...], lower[...]
    )
    eta_o[...] = eta
    blank = jnp.zeros((4, LANES), f32)
    up[0:2] = eta[0:2]
    up[2:4] = peta[0:2]
    up[4:8] = blank
    dn[0:2] = eta[CX - 2 : CX]
    dn[2:4] = peta[PX - 2 : PX]
    dn[4:8] = blank


def room_kernel(
    step, scal, inbox, windows, room, room_wet, face, door2, door_t2, fixed, near2, near_t2, near_index, near_gain,
    room_new, face_o, reply, etah_o, petah_o, eta_x, flux_x,
):
    received = inbox[...]
    flow = room_flow(received, windows[...], face[...])
    eta = room[0] + pick(door_t2[...], flow)
    eta, u, v = room_advance(eta, room[1], room[2], room_wet[step].astype(f32), eta_x, flux_x)
    room_new[0] = eta
    room_new[1] = u
    room_new[2] = v
    face_o[...], reply[...] = room_reply(eta, door2[...], fixed[...])
    tile = scal[0]
    left = inbox[pl.ds(pl.multiple_of(8 * lax.rem(tile + TILES - 1, TILES), 8), 8)]
    right = inbox[pl.ds(pl.multiple_of(8 * lax.rem(tile + 1, TILES), 8), 8)]
    at_lane = lane((8, LANES))

    def kept(cells):
        return jnp.where(jnp.where(lane(cells.shape) < R, TILES - 1 - tile, tile) > 0, cells, 0.0)

    petah_o[...] = kept(unpack4(left, right, L_PCOL, 2))
    eta_h = unpack4(left, right, L_CCOL, 8)
    spread = along(windows[...], L_WIN + ((jnp.where(at_lane < R, tile + 1, tile - 1)) & (TILES - 1)))
    target0 = jnp.where(at_lane < R, spread[0:1], spread[3:4])
    target1 = jnp.where(at_lane < R, spread[4:5], spread[7:8])
    eta_h = nudge(eta_h, jnp.concatenate([target0] * 4 + [target1] * 4, 0))
    levels = pick(near2[...], eta_h)
    sums = along(jnp.concatenate([received, received], 0), near_index[...])
    eta_h = eta_h - pick(near_t2[...], near_gain[...] * (4.0 * levels - sums))
    etah_o[...] = kept(eta_h)


def final_kernel(
    scal, inbox, eta, street, row_t2, index_a, gain, lower, u_x, v, peta, pu_x, pv, room, face, door_t2,
    parent_o, child_o, room_o,
):
    received = inbox[...]
    eta, windows = street_update(scal, received, eta[...], street[...], row_t2[...], index_a[...], gain[...], lower[...])
    child_o[0] = eta
    child_o[1] = u_x[8 : 8 + CX]
    child_o[2] = v[...]
    parent_o[0] = peta[...]
    parent_o[1] = pu_x[8 : 8 + PX]
    parent_o[2] = pv[...]
    room_o[0] = room[0] + pick(door_t2[...], room_flow(received, windows, face[...]))
    room_o[1] = room[1]
    room_o[2] = room[2]


def sds(*shape, dtype=f32):
    return jax.ShapeDtypeStruct(shape, dtype)


def call(name, kernel, outs, args, scalars=0, scratch=(), us=1, own_copies=False):
    spec = pl.BlockSpec(memory_space=pltpu.VMEM)
    first = pl.BlockSpec(memory_space=pltpu.HBM) if own_copies else spec
    scratch_shapes = [pltpu.VMEM((rows, LANES), f32) for rows in scratch]
    if own_copies:
        scratch_shapes = [pltpu.VMEM(a.shape, a.dtype) for a in args] + [pltpu.SemaphoreType.DMA((len(args),))]
    return pl.pallas_call(
        kernel,
        out_shape=outs,
        in_specs=[pl.BlockSpec(memory_space=pltpu.SMEM)] * scalars + [first] * (len(args) - scalars),
        out_specs=jax.tree.map(lambda _: spec, outs),
        scratch_shapes=scratch_shapes,
        compiler_params=pltpu.CompilerParams(vmem_limit_bytes=(60 if own_copies else 16) * 2**20),
        cost_estimate=pl.CostEstimate(flops=1000000 * us, bytes_accessed=1000000 * us, transcendentals=0),
        name=name,
    )(*args)


def shifts(up, dn, axis):
    count = lax.axis_size(axis)
    before = lax.ppermute(dn, axis, [(i, (i + 1) % count) for i in range(count)])
    after = lax.ppermute(up, axis, [((i + 1) % count, i) for i in range(count)])
    return before, after


def body(
    parent_state,
    parent_depth,
    child_state,
    child_depth,
    child_wet,
    interior_state,
    interior_wet,
    parent_anchor,
    open_row,
    open_col,
    open_owner,
    open_valid,
    open_conduct,
    door_rows,
):
    block, tall = sds(CX, LANES), sds(CX + 16, LANES)
    pblock, ptall = sds(PX, LANES), sds(PX + 16, LANES)
    grid, tile8, tile16 = sds(SLOTS, LANES), sds(8, LANES), sds(16, LANES)
    rooms = sds(3, CX, LANES)
    my_tile = lax.axis_index("tile").astype(i32)
    my_district = lax.axis_index("district").astype(i32)
    last = jnp.int32(lax.axis_size("district"))
    scal = jnp.stack([my_tile, parent_anchor[0, 0, 0], parent_anchor[0, 0, 1], my_district, last])

    def flat(values):
        return values.reshape(1, -1)

    up, dn, side = call(
        "edges",
        edges_kernel,
        [tile16] * 3,
        [
            parent_state, parent_depth, child_state, child_depth, child_wet, flat(open_row), flat(open_col),
            flat(open_owner), flat(open_valid), flat(open_conduct),
        ],
        own_copies=True,
    )
    above0, below0 = shifts(up, dn, "district")
    left0, right0 = shifts(side, side, "tile")
    row2, row_t2, index_s, index_a, gain, lower, fixed, door2, door_t2, room, face, reply = call(
        "setup",
        setup_kernel,
        [
            sds(SLOTS, LANES, dtype=bf16), sds(CX, 2 * SLOTS, dtype=bf16), sds(SLOTS, LANES, dtype=i32),
            sds(SLOTS, LANES, dtype=i32), grid, grid, grid, sds(SLOTS, LANES, dtype=bf16),
            sds(CX, 2 * SLOTS, dtype=bf16), rooms, grid, grid,
        ],
        [side, door_rows, interior_state, interior_wet],
        scratch=(CX + 16, CX + 16),
        us=4,
    )
    near = call(
        "near",
        near_kernel,
        [
            sds(2 * SLOTS, LANES, dtype=bf16), sds(CX, 4 * SLOTS, dtype=bf16), sds(2 * SLOTS, LANES, dtype=i32),
            sds(2 * SLOTS, LANES),
        ],
        [left0, right0],
        us=3,
    )
    outs = [block, tall, block, block, pblock, ptall, pblock, pblock, grid, grid]
    for step in range(STEPS):
        with_step = lambda *refs, step=step: send_kernel(step, *refs)
        if step == 0:
            args = [
                scal, parent_state, parent_depth, child_state, child_depth, child_wet, above0, below0, left0, right0,
                reply, row2, index_s,
            ]
            scratch = (CX + 16,) * 3 + (PX + 16,) * 3
        else:
            args = [
                scal, parent_depth, child_depth, child_wet, above0, below0, left0, right0, reply, row2, index_s,
                above, below, eta, u, v, v_h, eta_h, peta, pu, pv, pv_h, peta_h,
            ]
            scratch = (CX + 16,) * 2 + (PX + 16,) * 2
        eta, u, v, v_h, peta, pu, pv, pv_h, street, outbox = call(
            f"send{step}", with_step, outs, args, scalars=1, scratch=scratch
        )
        inbox = lax.all_to_all(outbox, "tile", split_axis=0, concat_axis=0, tiled=True)
        shared = [scal, inbox, eta, street, row_t2, index_a, gain, lower]
        if step == STEPS - 1:
            return tuple(
                call(
                    "final",
                    final_kernel,
                    [sds(3, PX, LANES), rooms, rooms],
                    shared + [u, v, peta, pu, pv, room, face, door_t2],
                    scalars=1,
                )
            )
        eta, up, dn, windows = call(
            f"street{step}", street_kernel, [block, tile8, tile8, tile8], shared + [peta], scalars=1
        )
        above, below = shifts(up, dn, "district")
        with_step = lambda *refs, step=step: room_kernel(step + 1, *refs)
        room, face, reply, eta_h, peta_h = call(
            f"room{step}",
            with_step,
            [rooms, grid, grid, block, pblock],
            [scal, inbox, windows, room, interior_wet, face, door2, door_t2, fixed, *near],
            scalars=1,
            scratch=(CX + 16, CX + 16),
            us=3,
        )


def solution(mesh):
    return jax.shard_map(
        body,
        mesh=mesh,
        in_specs=(
            P(None, "district", "tile"),
            P("district", "tile"),
            P(None, "district", "tile"),
            P("district", "tile"),
            P(None, "district", "tile"),
            P(None, ("district", "tile"), None),
            P(None, ("district", "tile"), None),
            P("district", None, None),
            P(("district", "tile")),
            P(("district", "tile")),
            P(("district", "tile"), None),
            P(("district", "tile")),
            P(("district", "tile")),
            P(("district", "tile"), None),
        ),
        out_specs=(
            P(None, "district", "tile"),
            P(None, "district", "tile"),
            P(None, ("district", "tile"), None),
        ),
        check_vma=False,
    )
```

```python
import jax
import jax.numpy as jnp
from jax import lax
from jax.experimental import pallas as pl
from jax.experimental.pallas import tpu as pltpu
from jax.sharding import PartitionSpec as P

f32 = jnp.float32
bf16 = jnp.bfloat16
i32 = jnp.int32

CX = 64
PX = 16
LANES = 128
R = 32
STEPS = 4
CAP = 8
TILES = 16
SLOTS = TILES * CAP

courant = 0.3
nudging = 0.25
area_ratio = 0.0625

L_ROOM = 32
L_NEAR = 64
L_FIX = 68
L_PCOL = 72
L_WIN = 80
L_CCOL = 96


def lane(shape):
    return lax.broadcasted_iota(i32, shape, 1)


def sub(shape):
    return lax.broadcasted_iota(i32, shape, 0)


def roll(cells, by):
    return pltpu.roll(cells, by % LANES, 1)


def along(cells, index):
    return jnp.take_along_axis(cells, index, axis=1, mode="promise_in_bounds")


def halves(cells):
    high = cells.astype(bf16)
    low = (cells - high.astype(f32)).astype(bf16)
    return jnp.concatenate([high, low], 0)


def pick(selector, cells):
    return jnp.dot(selector, halves(cells), preferred_element_type=f32)


def pack4(packed, cells, at):
    at_lane = lane(packed.shape)
    for g in range(cells.shape[0] // 8):
        first = at + 4 * g
        moved = roll(cells[8 * g : 8 * g + 8], first + 2)
        packed = jnp.where((at_lane >= first) & (at_lane < first + 4), moved, packed)
    return packed


def pack2(packed, cells, at):
    at_lane = lane(packed.shape)
    for g in range(cells.shape[0] // 8):
        first = at + 2 * g
        moved = roll(cells[8 * g : 8 * g + 8], first + 1)
        packed = jnp.where((at_lane >= first) & (at_lane < first + 2), moved, packed)
    return packed


def unpack4(left, right, at, groups):
    chosen = jnp.where(lane(left.shape) % 4 >= 2, right, left)
    return jnp.concatenate([roll(chosen, -(at + 4 * g + 2)) for g in range(groups)], 0)


def unpack2(left, right, at, groups):
    chosen = jnp.where(lane(left.shape) % 2 == 1, right, left)
    return jnp.concatenate([roll(chosen, -(at + 2 * g + 1)) for g in range(groups)], 0)


def advance(eta_x, u_x, v, v_h, eta_h, q, q_up, q_dn, q_h, flux_x, rows):
    top, end = 8, 8 + rows
    at_lane = lane((rows, LANES))
    first, last = at_lane == 0, at_lane == LANES - 1
    eta = eta_x[top:end]
    u_new = u_x[top:end] - courant * (eta_x[top + 1 : end + 1] - eta_x[top - 1 : end - 1])
    u_up = u_x[top - 1 : top] - courant * (eta_x[top : top + 1] - eta_x[top - 2 : top - 1])
    u_dn = u_x[end : end + 1] - courant * (eta_x[end + 1 : end + 2] - eta_x[end - 1 : end])
    after = roll(jnp.where(first, eta_h, eta), -1)
    before = roll(jnp.where(last, eta_h, eta), 1)
    v_new = v - courant * (after - before)
    after = roll(jnp.where(first, eta, eta_h), -1)
    before = roll(jnp.where(last, eta, eta_h), 1)
    v_edge = v_h - courant * (after - before)
    flux_x[top:end] = q * u_new
    flux_x[top - 1 : top] = q_up * u_up
    flux_x[end : end + 1] = q_dn * u_dn
    flux = q * v_new
    flux_h = q_h * v_edge
    after = roll(jnp.where(first, flux_h, flux), -1)
    before = roll(jnp.where(last, flux_h, flux), 1)
    eta_new = eta - courant * (
        flux_x[top + 1 : end + 1] - flux_x[top - 1 : end - 1] + after - before
    )
    return eta_new, u_new, u_up, u_dn, v_new, v_edge


def wet_of(q):
    return jnp.where(q > 0, 1.0, 0.0).astype(f32)


def room_advance(eta, u, v, wet, eta_x, flux_x):
    at_lane = lane((CX, LANES))
    first, last = at_lane == 0, at_lane == LANES - 1
    blank = jnp.zeros((8, LANES), f32)
    for ref in (eta_x, flux_x):
        ref[0:8] = blank
        ref[8 + CX : 16 + CX] = blank
    eta_x[8 : 8 + CX] = eta
    u_new = u - courant * (eta_x[9 : 9 + CX] - eta_x[7 : 7 + CX])
    v_new = v - courant * (
        jnp.where(last, 0.0, roll(eta, -1)) - jnp.where(first, 0.0, roll(eta, 1))
    )
    flux_x[8 : 8 + CX] = wet * u_new
    flux = wet * v_new
    eta_new = eta - courant * (
        flux_x[9 : 9 + CX]
        - flux_x[7 : 7 + CX]
        + jnp.where(last, 0.0, roll(flux, -1))
        - jnp.where(first, 0.0, roll(flux, 1))
    )
    return eta_new, wet * u_new, wet * v_new


def room_reply(eta, door2, fixed):
    sums = eta + roll(eta, -1)
    sums = sums + roll(sums, -2)
    at_lane = lane((CX, LANES))
    sums = along(sums, (4 * (at_lane - L_ROOM)) & (LANES - 1))
    both = pick(door2, jnp.concatenate([eta, sums], 1))
    rows, sums = both[:, :LANES], both[:, LANES:]
    ahead = roll(jnp.concatenate([sums[8:], sums[:8]], 0), L_NEAR - L_ROOM)
    behind = roll(jnp.concatenate([sums[-8:], sums[:-8]], 0), L_NEAR + 2 - (L_ROOM + 30))
    at_lane = lane(sums.shape)
    reply = jnp.where(
        at_lane < L_NEAR,
        sums,
        jnp.where(at_lane < L_NEAR + 2, ahead, jnp.where(at_lane < L_FIX, behind, fixed)),
    )
    return rows, reply


def slots_of(side):
    shape = (SLOTS, LANES)
    owner = jnp.broadcast_to(side[8:9], shape)
    earlier = (jnp.transpose(owner) == owner) & (sub(shape) < lane(shape))
    rank = jnp.sum(jnp.where(earlier, 1.0, 0.0), axis=0, keepdims=True)
    held = sub(shape).astype(f32) == jnp.where(side[8:9] >= 0, side[8:9] * CAP + rank, -1.0)

    def take(values):
        return jnp.sum(jnp.where(held, values, 0.0), axis=1, keepdims=True)

    row = take(side[9:10] + 1.0) - 1.0
    return row.astype(i32), take(side[10:11]).astype(i32), take(side[11:12])


def list_openings(side, row, col, owner, valid, conduct):
    count = owner.shape[1]
    side[8:9] = jnp.full((1, LANES), -1.0, f32)
    side[8:9, 0:count] = owner[...].astype(f32)
    side[9:10, 0:count] = row[...].astype(f32)
    side[10:11, 0:count] = col[...].astype(f32)
    side[11:12, 0:count] = conduct[...] * valid[...].astype(f32)


def edges_kernel(
    parent_i, parent_depth_i, child_i, child_depth_i, child_wet_i, row_i, col_i, owner_i, valid_i, conduct_i,
    up, dn, side,
    parent, parent_depth, child, child_depth, child_wet, row, col, owner, valid, conduct, done,
):
    pairs = [(child_wet_i.at[s], child_wet.at[s]) for s in range(STEPS)]
    pairs += [(child_i.at[f], child.at[f]) for f in (0, 2)]
    pairs += [(child_i.at[1, pl.ds(r, 8)], child.at[1, pl.ds(r, 8)]) for r in (0, CX - 8)]
    pairs += [
        (child_depth_i, child_depth), (parent_i, parent), (parent_depth_i, parent_depth),
        (row_i, row), (col_i, col), (owner_i, owner), (valid_i, valid), (conduct_i, conduct),
    ]
    copies = [pltpu.make_async_copy(src, dst, done.at[k]) for k, (src, dst) in enumerate(pairs)]
    for copy in copies:
        copy.start()
    up[...] = jnp.zeros((16, LANES), f32)
    dn[...] = jnp.zeros((16, LANES), f32)
    side[...] = jnp.zeros((16, LANES), f32)
    for copy in copies:
        copy.wait()
    eta = child[0]
    packed = pack4(jnp.zeros((8, LANES), f32), eta, 0)
    packed = pack2(packed, child[2], 32)
    up[0:2] = eta[0:2]
    dn[0:2] = eta[CX - 2 : CX]
    up[2:3] = child[1, 0:1]
    dn[2:3] = child[1, CX - 1 : CX]
    for s in range(STEPS):
        q = child_depth[...] * child_wet[s].astype(f32)
        up[3 + s : 4 + s] = q[0:1]
        dn[3 + s : 4 + s] = q[CX - 1 : CX]
        packed = pack2(packed, q, 48 + 16 * s)
    eta = parent[0]
    up[7:9] = eta[0:2]
    dn[7:9] = eta[PX - 2 : PX]
    up[9:10] = parent[1, 0:1]
    dn[9:10] = parent[1, PX - 1 : PX]
    up[10:11] = parent_depth[0:1]
    dn[10:11] = parent_depth[PX - 1 : PX]
    packed = pack4(packed, eta, 112)
    packed = pack2(packed, parent[2], 120)
    packed = pack2(packed, parent_depth[...], 124)
    side[0:8] = packed
    list_openings(side, row, col, owner, valid, conduct)


def setup_kernel(
    opening_row, opening_col, owner, valid, conduct, anchor, door, room, room_wet, row2, row_t2, index_s, index_a, gain, lower, fixed,
    door2, door_t2, room_new, face, reply, place, eta_x, flux_x, side,
):
    side[8:16] = jnp.zeros((8, LANES), f32)
    list_openings(side, opening_row, opening_col, owner, valid, conduct)
    place[0:8] = jnp.broadcast_to(anchor[0:1, 0:1], (8, LANES))
    place[8:16] = jnp.broadcast_to(anchor[1:2, 0:1], (8, LANES))
    shape = (SLOTS, LANES)
    at_lane = lane(shape)
    row, col, weight = slots_of(side[...])
    chosen = jnp.where(at_lane == row, 1.0, 0.0)
    row2[...] = (chosen + roll(chosen, CX)).astype(bf16)
    turned = jnp.transpose(chosen)[0:CX].astype(bf16)
    row_t2[...] = jnp.concatenate([turned, turned], 1)
    index_s[...] = (at_lane + col) & (LANES - 1)
    index_a[...] = (at_lane - col + L_ROOM) & (LANES - 1)
    inside = (at_lane >= col) & (at_lane < col + R)
    gain[...] = jnp.where(inside, area_ratio * weight, 0.0)
    half = jnp.where(row >= R, 1.0, 0.0)
    lower[...] = jnp.broadcast_to(half, shape)
    fixed_now = jnp.where(
        at_lane == L_FIX,
        weight,
        jnp.where(at_lane == L_FIX + 1, col.astype(f32), jnp.where(at_lane == L_FIX + 2, half, 0.0)),
    )
    fixed[...] = fixed_now
    chosen_t = jnp.where(sub(shape) == door[...], 1.0, 0.0)
    turned = chosen_t[0:CX].astype(bf16)
    door_t2[...] = jnp.concatenate([turned, turned], 1)
    chosen = jnp.transpose(chosen_t)
    both = (chosen + roll(chosen, CX)).astype(bf16)
    door2[...] = both
    eta, u, v = room_advance(room[0], room[1], room[2], room_wet[0].astype(f32), eta_x, flux_x)
    room_new[0] = eta
    room_new[1] = u
    room_new[2] = v
    face[...], reply[...] = room_reply(eta, both, fixed_now)


def near_kernel(left, right, row2, row_t2, index, gain):
    shape = (SLOTS, LANES)
    at_lane = lane(shape)
    turned = []
    for part, side in enumerate((right, left)):
        rows = slice(part * SLOTS, (part + 1) * SLOTS)
        row, col, weight = slots_of(side[...])
        chosen = jnp.where(at_lane == row, 1.0, 0.0)
        row2[rows] = (chosen + roll(chosen, CX)).astype(bf16)
        turned.append(jnp.transpose(chosen)[0:CX].astype(bf16))
        if part == 0:
            touched = (at_lane < 2) & (at_lane >= col)
            index[rows] = (at_lane - col + L_NEAR) & (LANES - 1)
        else:
            touched = (at_lane >= LANES - 2) & (at_lane < col + R)
            index[rows] = (at_lane - col + (L_NEAR + 2 - 30)) & (LANES - 1)
        gain[rows] = jnp.where(touched, area_ratio * weight, 0.0)
    row_t2[...] = jnp.concatenate(turned + turned, 1)


def gate(there, cells):
    return jnp.where(there, cells, 0.0)


def send_kernel(step, *refs):
    tile, district = lax.axis_index("tile"), lax.axis_index("district")
    has_left, has_right = tile > 0, tile < TILES - 1
    has_above, has_below = district > 0, district < lax.axis_size("district") - 1
    last = step == STEPS - 1
    if step == 0:
        (
            place, parent, parent_depth, child, child_depth, child_wet, above0, below0, left0, right0, reply, row2, index_s,
            eta_o, u_o, v_o, peta_o, pu_o, pv_o, street_o, out, *more, eta_x, flux_x, u_x, peta_x, pflux_x, pu_x,
        ) = refs
        u_x[8 : 8 + CX] = child[1]
        u_x[7:8] = gate(has_above, above0[2:3])
        u_x[8 + CX : 9 + CX] = gate(has_below, below0[2:3])
        pu_x[8 : 8 + PX] = parent[1]
        pu_x[7:8] = gate(has_above, above0[9:10])
        pu_x[8 + PX : 9 + PX] = gate(has_below, below0[9:10])
        eta_x[8 : 8 + CX] = child[0]
        peta_x[8 : 8 + PX] = parent[0]
        eta_x[6:8] = gate(has_above, above0[0:2])
        eta_x[8 + CX : 10 + CX] = gate(has_below, below0[0:2])
        peta_x[6:8] = gate(has_above, above0[7:9])
        peta_x[8 + PX : 10 + PX] = gate(has_below, below0[7:9])
        left, right = gate(has_left, left0[0:8]), gate(has_right, right0[0:8])
        v, v_h = child[2], unpack2(left, right, 32, 8)
        eta_h = unpack4(left, right, 0, 8)
        pv, pv_h = parent[2], unpack2(left, right, 120, 2)
        peta_h = unpack4(left, right, 112, 2)
    else:
        (
            place, parent_depth, child_depth, child_wet, above0, below0, left0, right0, reply, row2, index_s,
            above, below, eta_i, u_x, v_i, vh_i, etah_i, peta_i, pu_x, pv_i, pvh_i, petah_i,
            eta_o, u_o, v_o, peta_o, pu_o, pv_o, street_o, out, *more, eta_x, flux_x, peta_x, pflux_x,
        ) = refs
        eta_x[8 : 8 + CX] = eta_i[...]
        peta_x[8 : 8 + PX] = peta_i[...]
        eta_x[6:8] = gate(has_above, above[0:2])
        eta_x[8 + CX : 10 + CX] = gate(has_below, below[0:2])
        peta_x[6:8] = gate(has_above, above[2:4])
        peta_x[8 + PX : 10 + PX] = gate(has_below, below[2:4])
        left, right = gate(has_left, left0[0:8]), gate(has_right, right0[0:8])
        v, v_h, eta_h = v_i[...], vh_i[...], etah_i[...]
        pv, pv_h, peta_h = pv_i[...], pvh_i[...], petah_i[...]
    wet = child_wet[step].astype(f32)
    q = child_depth[...] * wet
    q_up = gate(has_above, above0[3 + step : 4 + step])
    q_dn = gate(has_below, below0[3 + step : 4 + step])
    pq_up, pq_dn = gate(has_above, above0[10:11]), gate(has_below, below0[10:11])
    q_h = unpack2(left, right, 48 + 16 * step, 8)
    eta, u, u_up, u_dn, v, v_h = advance(eta_x, u_x, v, v_h, eta_h, q, q_up, q_dn, q_h, flux_x, CX)
    street = pick(row2[...], eta)
    peta, pu, pu_up, pu_dn, pv, pv_h = advance(
        peta_x, pu_x, pv, pv_h, peta_h, parent_depth[...], pq_up, pq_dn, unpack2(left, right, 124, 2), pflux_x, PX
    )
    eta_o[...] = eta
    u_o[8 : 8 + CX] = wet * u
    v_o[...] = wet * v
    peta_o[...] = peta
    pu_o[8 : 8 + PX] = pu
    pv_o[...] = pv
    street_o[...] = street
    if not last:
        vh_o, pvh_o = more
        u_o[7:8] = wet_of(q_up) * u_up
        u_o[8 + CX : 9 + CX] = wet_of(q_dn) * u_dn
        vh_o[...] = wet_of(q_h) * v_h
        pu_o[7:8] = pu_up
        pu_o[8 + PX : 9 + PX] = pu_dn
        pvh_o[...] = pv_h
    shape = (8, LANES)
    at_lane = lane(shape)
    common = pack4(jnp.zeros(shape, f32), eta, L_CCOL)
    common = pack4(common, peta, L_PCOL)
    first_row, first_col = place[0:8], place[8:16]
    lines = []
    for k in range(2):
        halves_of = [jnp.where(sub(shape) + g == first_row + k, peta[g : g + 8], 0.0) for g in (0, 8)]
        lines.append(jnp.sum(halves_of[0] + halves_of[1], axis=0, keepdims=True))
    lines = jnp.where(sub(shape) < 4, lines[0], lines[1])
    index = first_col - LANES * tile + 4 * (at_lane - L_WIN) + (sub(shape) & 3)
    window = along(lines, index & (LANES - 1))
    window = jnp.where((index >= 0) & (index < LANES), window, 0.0)
    common = jnp.where((at_lane >= L_WIN) & (at_lane < L_CCOL), window, common)
    street = along(street, index_s[...])
    for t in range(TILES):
        rows = slice(t * CAP, (t + 1) * CAP)
        out[rows] = jnp.where(at_lane < R, street[rows], jnp.where(at_lane < L_PCOL, reply[rows], common))


def windows_sum(inbox):
    parts = [inbox[8 * t : 8 * t + 8] for t in range(TILES)]
    while len(parts) > 1:
        parts = [parts[i] + parts[i + 1] for i in range(0, len(parts), 2)]
    return parts[0]


def nudge(eta, target):
    return eta + nudging * (target - eta)


def street_update(inbox, eta, street, row_t2, index_a, gain, lower):
    shape = (8, LANES)
    windows = windows_sum(inbox)
    mine = along(windows, jnp.full(shape, L_WIN, i32) + lax.axis_index("tile"))
    mine = jnp.where((sub(shape) & 3) == lane(shape) // R, mine, 0.0)
    target0 = jnp.sum(mine[0:4], axis=0, keepdims=True)
    target1 = jnp.sum(mine[4:8], axis=0, keepdims=True)
    eta = jnp.concatenate([nudge(eta[0:R], target0), nudge(eta[R:CX], target1)], 0)
    levels = nudge(street, jnp.where(lower > 0, target1, target0))
    flow = gain * (4.0 * levels - along(inbox, index_a))
    return eta - pick(row_t2, flow), windows


def room_flow(inbox, windows, face):
    shape = (SLOTS, LANES)
    at_lane = lane(shape)
    holder = jnp.where(at_lane == L_WIN + sub(shape) // CAP, 1.0, 0.0).astype(bf16)
    high = windows.astype(bf16)
    low = (windows - high.astype(f32)).astype(bf16)
    per_slot = lax.dot_general(
        jnp.concatenate([holder, holder], 1),
        jnp.concatenate([jnp.concatenate([high, low], 1), jnp.zeros((LANES - 8, 2 * LANES), bf16)], 0),
        (((1,), (1,)), ((), ())),
        preferred_element_type=f32,
    )
    weight = inbox[:, L_FIX : L_FIX + 1]
    col = inbox[:, L_FIX + 1 : L_FIX + 2].astype(i32)
    half = inbox[:, L_FIX + 2 : L_FIX + 3].astype(i32)
    cell = at_lane // 4
    target = along(per_slot, 4 * half + ((col + cell) // R & 3))
    levels = nudge(along(inbox, cell), target)
    return weight * (levels - face)


def street_kernel(inbox, eta, street, row_t2, index_a, gain, lower, peta, eta_o, up, dn, windows_o):
    eta, windows_o[...] = street_update(
        inbox[...], eta[...], street[...], row_t2[...], index_a[...], gain[...], lower[...]
    )
    eta_o[...] = eta
    blank = jnp.zeros((4, LANES), f32)
    up[0:2] = eta[0:2]
    up[2:4] = peta[0:2]
    up[4:8] = blank
    dn[0:2] = eta[CX - 2 : CX]
    dn[2:4] = peta[PX - 2 : PX]
    dn[4:8] = blank


def room_kernel(
    step, inbox, windows, room, room_wet, face, door2, door_t2, fixed, near2, near_t2, near_index, near_gain,
    room_new, face_o, reply, etah_o, petah_o, eta_x, flux_x,
):
    received = inbox[...]
    flow = room_flow(received, windows[...], face[...])
    eta = room[0] + pick(door_t2[...], flow)
    eta, u, v = room_advance(eta, room[1], room[2], room_wet[step].astype(f32), eta_x, flux_x)
    room_new[0] = eta
    room_new[1] = u
    room_new[2] = v
    face_o[...], reply[...] = room_reply(eta, door2[...], fixed[...])
    tile = lax.axis_index("tile")
    left = inbox[pl.ds(pl.multiple_of(8 * lax.rem(tile + TILES - 1, TILES), 8), 8)]
    right = inbox[pl.ds(pl.multiple_of(8 * lax.rem(tile + 1, TILES), 8), 8)]
    at_lane = lane((8, LANES))

    def kept(cells):
        return jnp.where(jnp.where(lane(cells.shape) < R, TILES - 1 - tile, tile) > 0, cells, 0.0)

    petah_o[...] = kept(unpack4(left, right, L_PCOL, 2))
    eta_h = unpack4(left, right, L_CCOL, 8)
    spread = along(windows[...], L_WIN + ((jnp.where(at_lane < R, tile + 1, tile - 1)) & (TILES - 1)))
    target0 = jnp.where(at_lane < R, spread[0:1], spread[3:4])
    target1 = jnp.where(at_lane < R, spread[4:5], spread[7:8])
    eta_h = nudge(eta_h, jnp.concatenate([target0] * 4 + [target1] * 4, 0))
    levels = pick(near2[...], eta_h)
    sums = along(jnp.concatenate([received, received], 0), near_index[...])
    eta_h = eta_h - pick(near_t2[...], near_gain[...] * (4.0 * levels - sums))
    etah_o[...] = kept(eta_h)


def final_kernel(
    inbox, eta, street, row_t2, index_a, gain, lower, u_x, v, peta, pu_x, pv, room, face, door_t2,
    parent_o, child_o, room_o, child_eta, room_eta, done,
):
    pairs = [
        (u_x.at[pl.ds(8, CX)], child_o.at[1]), (v, child_o.at[2]), (peta, parent_o.at[0]),
        (pu_x.at[pl.ds(8, PX)], parent_o.at[1]), (pv, parent_o.at[2]), (room.at[1], room_o.at[1]),
        (room.at[2], room_o.at[2]), (room_eta, room_o.at[0]), (child_eta, child_o.at[0]),
    ]
    copies = [pltpu.make_async_copy(src, dst, done.at[k]) for k, (src, dst) in enumerate(pairs)]
    for copy in copies[:-2]:
        copy.start()
    received = inbox[...]
    child_eta[...], windows = street_update(
        received, eta[...], street[...], row_t2[...], index_a[...], gain[...], lower[...]
    )
    copies[-1].start()
    room_eta[...] = room[0] + pick(door_t2[...], room_flow(received, windows, face[...]))
    copies[-2].start()
    for copy in copies:
        copy.wait()


def sds(*shape, dtype=f32):
    return jax.ShapeDtypeStruct(shape, dtype)


VMEM = pl.BlockSpec(memory_space=pltpu.VMEM)
HBM = pl.BlockSpec(memory_space=pltpu.HBM)


def call(name, kernel, outs, args, scratch=(), us=1, reads=VMEM, writes=VMEM, limit=16):
    return pl.pallas_call(
        kernel,
        out_shape=outs,
        in_specs=[reads] * len(args),
        out_specs=[writes] * len(outs),
        scratch_shapes=[pltpu.VMEM((rows, LANES), f32) if isinstance(rows, int) else rows for rows in scratch],
        compiler_params=pltpu.CompilerParams(vmem_limit_bytes=limit * 2**20),
        cost_estimate=pl.CostEstimate(flops=1000000 * us, bytes_accessed=1000000 * us, transcendentals=0),
        name=name,
    )(*args)


def to_next(cells, axis):
    count = lax.axis_size(axis)
    return lax.ppermute(cells, axis, [(i, (i + 1) % count) for i in range(count)])


def to_previous(cells, axis):
    count = lax.axis_size(axis)
    return lax.ppermute(cells, axis, [((i + 1) % count, i) for i in range(count)])


def body(
    parent_state,
    parent_depth,
    child_state,
    child_depth,
    child_wet,
    interior_state,
    interior_wet,
    parent_anchor,
    open_row,
    open_col,
    open_owner,
    open_valid,
    open_conduct,
    door_rows,
):
    block, tall = sds(CX, LANES), sds(CX + 16, LANES)
    pblock, ptall = sds(PX, LANES), sds(PX + 16, LANES)
    grid, tile8, tile16 = sds(SLOTS, LANES), sds(8, LANES), sds(16, LANES)
    rooms = sds(3, CX, LANES)

    def flat(values):
        return values.reshape(1, -1)

    openings = [flat(open_row), flat(open_col), flat(open_owner), flat(open_valid), flat(open_conduct)]
    inputs = [parent_state, parent_depth, child_state, child_depth, child_wet, *openings]
    up, dn, side = call(
        "edges",
        edges_kernel,
        [tile16] * 3,
        inputs,
        scratch=[pltpu.VMEM(a.shape, a.dtype) for a in inputs] + [pltpu.SemaphoreType.DMA((16,))],
        reads=HBM,
        limit=60,
    )
    left0 = to_next(side, "tile")
    right0 = to_previous(side, "tile")
    row2, row_t2, index_s, index_a, gain, lower, fixed, door2, door_t2, room, face, reply, place = call(
        "setup",
        setup_kernel,
        [
            sds(SLOTS, LANES, dtype=bf16), sds(CX, 2 * SLOTS, dtype=bf16), sds(SLOTS, LANES, dtype=i32),
            sds(SLOTS, LANES, dtype=i32), grid, grid, grid, sds(SLOTS, LANES, dtype=bf16),
            sds(CX, 2 * SLOTS, dtype=bf16), rooms, grid, grid, sds(16, LANES, dtype=i32),
        ],
        [*openings, jnp.transpose(parent_anchor, (0, 2, 1))[0], door_rows, interior_state, interior_wet],
        scratch=(CX + 16, CX + 16, 16),
    )
    above0 = to_next(dn, "district")
    below0 = to_previous(up, "district")
    near = call(
        "near",
        near_kernel,
        [
            sds(2 * SLOTS, LANES, dtype=bf16), sds(CX, 4 * SLOTS, dtype=bf16), sds(2 * SLOTS, LANES, dtype=i32),
            sds(2 * SLOTS, LANES),
        ],
        [left0, right0],
    )
    for step in range(STEPS):
        with_step = lambda *refs, step=step: send_kernel(step, *refs)
        if step == 0:
            args = [
                place, parent_state, parent_depth, child_state, child_depth, child_wet, above0, below0, left0, right0,
                reply, row2, index_s,
            ]
            scratch = (CX + 16,) * 3 + (PX + 16,) * 3
        else:
            args = [
                place, parent_depth, child_depth, child_wet, above0, below0, left0, right0, reply, row2, index_s,
                above, below, eta, u, v, v_h, eta_h, peta, pu, pv, pv_h, peta_h,
            ]
            scratch = (CX + 16,) * 2 + (PX + 16,) * 2
        outs = [block, tall, block, pblock, ptall, pblock, grid, grid]
        if step < STEPS - 1:
            outs += [block, pblock]
        eta, u, v, peta, pu, pv, street, outbox, *more = call(f"send{step}", with_step, outs, args, scratch=scratch)
        inbox = lax.all_to_all(outbox, "tile", split_axis=0, concat_axis=0, tiled=True)
        shared = [inbox, eta, street, row_t2, index_a, gain, lower]
        if step == STEPS - 1:
            return tuple(
                call(
                    "final",
                    final_kernel,
                    [sds(3, PX, LANES), rooms, rooms],
                    shared + [u, v, peta, pu, pv, room, face, door_t2],
                    scratch=(CX, CX, pltpu.SemaphoreType.DMA((9,))),
                    writes=HBM,
                )
            )
        v_h, pv_h = more
        eta, up, dn, windows = call(f"street{step}", street_kernel, [block, tile8, tile8, tile8], shared + [peta])
        below = to_previous(up, "district")
        above = to_next(dn, "district")
        with_step = lambda *refs, step=step: room_kernel(step + 1, *refs)
        room, face, reply, eta_h, peta_h = call(
            f"room{step}",
            with_step,
            [rooms, grid, grid, block, pblock],
            [inbox, windows, room, interior_wet, face, door2, door_t2, fixed, *near],
            scratch=(CX + 16, CX + 16),
        )


def solution(mesh):
    return jax.shard_map(
        body,
        mesh=mesh,
        in_specs=(
            P(None, "district", "tile"),
            P("district", "tile"),
            P(None, "district", "tile"),
            P("district", "tile"),
            P(None, "district", "tile"),
            P(None, ("district", "tile"), None),
            P(None, ("district", "tile"), None),
            P("district", None, None),
            P(("district", "tile")),
            P(("district", "tile")),
            P(("district", "tile"), None),
            P(("district", "tile")),
            P(("district", "tile")),
            P(("district", "tile"), None),
        ),
        out_specs=(
            P(None, "district", "tile"),
            P(None, "district", "tile"),
            P(None, ("district", "tile"), None),
        ),
        check_vma=False,
    )
```

```python
import jax
import jax.numpy as jnp
from jax import lax
from jax.experimental import pallas as pl
from jax.experimental.pallas import tpu as pltpu
from jax.sharding import PartitionSpec as P

f32 = jnp.float32
bf16 = jnp.bfloat16
i32 = jnp.int32

CX = 64
PX = 16
LANES = 128
R = 32
STEPS = 4
CAP = 8
TILES = 16
SLOTS = TILES * CAP

courant = 0.3
nudging = 0.25
area_ratio = 0.0625

L_ROOM = 32
L_NEAR = 64
L_FIX = 68
L_PCOL = 72
L_WIN = 80
L_CCOL = 96
L_CROW = 64
L_PROW = 96


def lane(shape):
    return lax.broadcasted_iota(i32, shape, 1)


def sub(shape):
    return lax.broadcasted_iota(i32, shape, 0)


def roll(cells, by):
    return pltpu.roll(cells, by % LANES, 1)


def along(cells, index):
    return jnp.take_along_axis(cells, index, axis=1, mode="promise_in_bounds")


def halves(cells):
    high = cells.astype(bf16)
    low = (cells - high.astype(f32)).astype(bf16)
    return jnp.concatenate([high, low], 0)


def pick(selector, cells):
    return jnp.dot(selector, halves(cells), preferred_element_type=f32)


def pack4(packed, cells, at):
    at_lane = lane(packed.shape)
    for g in range(cells.shape[0] // 8):
        first = at + 4 * g
        moved = roll(cells[8 * g : 8 * g + 8], first + 2)
        packed = jnp.where((at_lane >= first) & (at_lane < first + 4), moved, packed)
    return packed


def pack2(packed, cells, at):
    at_lane = lane(packed.shape)
    for g in range(cells.shape[0] // 8):
        first = at + 2 * g
        moved = roll(cells[8 * g : 8 * g + 8], first + 1)
        packed = jnp.where((at_lane >= first) & (at_lane < first + 2), moved, packed)
    return packed


def unpack4(left, right, at, groups):
    chosen = jnp.where(lane(left.shape) % 4 >= 2, right, left)
    return jnp.concatenate([roll(chosen, -(at + 4 * g + 2)) for g in range(groups)], 0)


def unpack2(left, right, at, groups):
    chosen = jnp.where(lane(left.shape) % 2 == 1, right, left)
    return jnp.concatenate([roll(chosen, -(at + 2 * g + 1)) for g in range(groups)], 0)


def pack_rows(packed, rows, at):
    shape = packed.shape
    both = jnp.where(sub(shape) < 4, rows[0:1], rows[1:2])
    inside = (lane(shape) >= at) & (lane(shape) < at + R)
    for k in range(4):
        packed = jnp.where(inside & ((sub(shape) & 3) == k), roll(both, at - R * k), packed)
    return packed


def unpack_rows(packed, at):
    shape = packed.shape
    spread = jnp.zeros(shape, f32)
    for k in range(4):
        spread = jnp.where(((sub(shape) & 3) == k) & (lane(shape) // R == k), roll(packed, R * k - at), spread)
    return jnp.sum(spread[0:4], axis=0, keepdims=True), jnp.sum(spread[4:8], axis=0, keepdims=True)


def odd_tile():
    return lax.rem(lax.axis_index("tile"), 2) == 1


def sibling():
    tile = lax.axis_index("tile")
    return tile + 1 - 2 * lax.rem(tile, 2)


def for_me(inbox):
    return inbox[:, 0:CAP].reshape(SLOTS, LANES)


def advance(eta_x, u_x, v, v_h, eta_h, q, q_up, q_dn, q_h, flux_x, rows):
    top, end = 8, 8 + rows
    at_lane = lane((rows, LANES))
    first, last = at_lane == 0, at_lane == LANES - 1
    eta = eta_x[top:end]
    u_new = u_x[top:end] - courant * (eta_x[top + 1 : end + 1] - eta_x[top - 1 : end - 1])
    u_up = u_x[top - 1 : top] - courant * (eta_x[top : top + 1] - eta_x[top - 2 : top - 1])
    u_dn = u_x[end : end + 1] - courant * (eta_x[end + 1 : end + 2] - eta_x[end - 1 : end])
    after = roll(jnp.where(first, eta_h, eta), -1)
    before = roll(jnp.where(last, eta_h, eta), 1)
    v_new = v - courant * (after - before)
    after = roll(jnp.where(first, eta, eta_h), -1)
    before = roll(jnp.where(last, eta, eta_h), 1)
    v_edge = v_h - courant * (after - before)
    flux_x[top:end] = q * u_new
    flux_x[top - 1 : top] = q_up * u_up
    flux_x[end : end + 1] = q_dn * u_dn
    flux = q * v_new
    flux_h = q_h * v_edge
    after = roll(jnp.where(first, flux_h, flux), -1)
    before = roll(jnp.where(last, flux_h, flux), 1)
    eta_new = eta - courant * (
        flux_x[top + 1 : end + 1] - flux_x[top - 1 : end - 1] + after - before
    )
    return eta_new, u_new, u_up, u_dn, v_new, v_edge


def wet_of(q):
    return jnp.where(q > 0, 1.0, 0.0).astype(f32)


def room_advance(eta, u, v, wet, eta_x, flux_x):
    at_lane = lane((CX, LANES))
    first, last = at_lane == 0, at_lane == LANES - 1
    blank = jnp.zeros((8, LANES), f32)
    for ref in (eta_x, flux_x):
        ref[0:8] = blank
        ref[8 + CX : 16 + CX] = blank
    eta_x[8 : 8 + CX] = eta
    u_new = u - courant * (eta_x[9 : 9 + CX] - eta_x[7 : 7 + CX])
    v_new = v - courant * (
        jnp.where(last, 0.0, roll(eta, -1)) - jnp.where(first, 0.0, roll(eta, 1))
    )
    flux_x[8 : 8 + CX] = wet * u_new
    flux = wet * v_new
    eta_new = eta - courant * (
        flux_x[9 : 9 + CX]
        - flux_x[7 : 7 + CX]
        + jnp.where(last, 0.0, roll(flux, -1))
        - jnp.where(first, 0.0, roll(flux, 1))
    )
    return eta_new, wet * u_new, wet * v_new


def room_reply(eta, door2, fixed):
    sums = eta + roll(eta, -1)
    sums = sums + roll(sums, -2)
    at_lane = lane((CX, LANES))
    sums = along(sums, (4 * (at_lane - L_ROOM)) & (LANES - 1))
    both = pick(door2, jnp.concatenate([eta, sums], 1))
    rows, sums = both[:, :LANES], both[:, LANES:]
    ahead = roll(jnp.concatenate([sums[8:], sums[:8]], 0), L_NEAR - L_ROOM)
    behind = roll(jnp.concatenate([sums[-8:], sums[:-8]], 0), L_NEAR + 2 - (L_ROOM + 30))
    at_lane = lane(sums.shape)
    reply = jnp.where(
        at_lane < L_NEAR,
        sums,
        jnp.where(at_lane < L_NEAR + 2, ahead, jnp.where(at_lane < L_FIX, behind, fixed)),
    )
    return rows, reply


def slots_of(side):
    shape = (SLOTS, LANES)
    owner = jnp.broadcast_to(side[8:9], shape)
    earlier = (jnp.transpose(owner) == owner) & (sub(shape) < lane(shape))
    rank = jnp.sum(jnp.where(earlier, 1.0, 0.0), axis=0, keepdims=True)
    held = sub(shape).astype(f32) == jnp.where(side[8:9] >= 0, side[8:9] * CAP + rank, -1.0)

    def take(values):
        return jnp.sum(jnp.where(held, values, 0.0), axis=1, keepdims=True)

    row = take(side[9:10] + 1.0) - 1.0
    return row.astype(i32), take(side[10:11]).astype(i32), take(side[11:12])


def list_openings(side, row, col, owner, valid, conduct):
    count = owner.shape[1]
    side[8:9] = jnp.full((1, LANES), -1.0, f32)
    side[8:9, 0:count] = owner[...].astype(f32)
    side[9:10, 0:count] = row[...].astype(f32)
    side[10:11, 0:count] = col[...].astype(f32)
    side[11:12, 0:count] = conduct[...] * valid[...].astype(f32)


def edges_kernel(
    parent_i, parent_depth_i, child_i, child_depth_i, child_wet_i, row_i, col_i, owner_i, valid_i, conduct_i,
    up, dn, side,
    parent, parent_depth, child, child_depth, child_wet, row, col, owner, valid, conduct, done,
):
    pairs = [(child_wet_i.at[s], child_wet.at[s]) for s in range(STEPS)]
    pairs += [(child_i.at[f], child.at[f]) for f in (0, 2)]
    pairs += [(child_i.at[1, pl.ds(r, 8)], child.at[1, pl.ds(r, 8)]) for r in (0, CX - 8)]
    pairs += [
        (child_depth_i, child_depth), (parent_i, parent), (parent_depth_i, parent_depth),
        (row_i, row), (col_i, col), (owner_i, owner), (valid_i, valid), (conduct_i, conduct),
    ]
    copies = [pltpu.make_async_copy(src, dst, done.at[k]) for k, (src, dst) in enumerate(pairs)]
    for copy in copies:
        copy.start()
    up[...] = jnp.zeros((16, LANES), f32)
    dn[...] = jnp.zeros((16, LANES), f32)
    side[...] = jnp.zeros((16, LANES), f32)
    for copy in copies:
        copy.wait()
    eta = child[0]
    packed = pack4(jnp.zeros((8, LANES), f32), eta, 0)
    packed = pack2(packed, child[2], 32)
    up[0:2] = eta[0:2]
    dn[0:2] = eta[CX - 2 : CX]
    up[2:3] = child[1, 0:1]
    dn[2:3] = child[1, CX - 1 : CX]
    for s in range(STEPS):
        q = child_depth[...] * child_wet[s].astype(f32)
        up[3 + s : 4 + s] = q[0:1]
        dn[3 + s : 4 + s] = q[CX - 1 : CX]
        packed = pack2(packed, q, 48 + 16 * s)
    eta = parent[0]
    up[7:9] = eta[0:2]
    dn[7:9] = eta[PX - 2 : PX]
    up[9:10] = parent[1, 0:1]
    dn[9:10] = parent[1, PX - 1 : PX]
    up[10:11] = parent_depth[0:1]
    dn[10:11] = parent_depth[PX - 1 : PX]
    packed = pack4(packed, eta, 112)
    packed = pack2(packed, parent[2], 120)
    packed = pack2(packed, parent_depth[...], 124)
    side[0:8] = packed
    list_openings(side, row, col, owner, valid, conduct)


def setup_kernel(
    opening_row, opening_col, owner, valid, conduct, anchor, door, room, room_wet, row2, row_t2, index_s, index_a, gain, lower, fixed,
    door2, door_t2, room_new, face, reply, place, eta_x, flux_x, side,
):
    side[8:16] = jnp.zeros((8, LANES), f32)
    list_openings(side, opening_row, opening_col, owner, valid, conduct)
    place[0:8] = jnp.broadcast_to(anchor[0:1, 0:1], (8, LANES))
    place[8:16] = jnp.broadcast_to(anchor[1:2, 0:1], (8, LANES))
    shape = (SLOTS, LANES)
    at_lane = lane(shape)
    row, col, weight = slots_of(side[...])
    chosen = jnp.where(at_lane == row, 1.0, 0.0)
    row2[...] = (chosen + roll(chosen, CX)).astype(bf16)
    turned = jnp.transpose(chosen)[0:CX].astype(bf16)
    row_t2[...] = jnp.concatenate([turned, turned], 1)
    index_s[...] = (at_lane + col) & (LANES - 1)
    index_a[...] = (at_lane - col + L_ROOM) & (LANES - 1)
    inside = (at_lane >= col) & (at_lane < col + R)
    gain[...] = jnp.where(inside, area_ratio * weight, 0.0)
    half = jnp.where(row >= R, 1.0, 0.0)
    lower[...] = jnp.broadcast_to(half, shape)
    fixed_now = jnp.where(
        at_lane == L_FIX,
        weight,
        jnp.where(at_lane == L_FIX + 1, col.astype(f32), jnp.where(at_lane == L_FIX + 2, half, 0.0)),
    )
    fixed[...] = fixed_now
    chosen_t = jnp.where(sub(shape) == door[...], 1.0, 0.0)
    turned = chosen_t[0:CX].astype(bf16)
    door_t2[...] = jnp.concatenate([turned, turned], 1)
    chosen = jnp.transpose(chosen_t)
    both = (chosen + roll(chosen, CX)).astype(bf16)
    door2[...] = both
    eta, u, v = room_advance(room[0], room[1], room[2], room_wet[0].astype(f32), eta_x, flux_x)
    room_new[0] = eta
    room_new[1] = u
    room_new[2] = v
    face[...], reply[...] = room_reply(eta, both, fixed_now)


def near_kernel(first, second, row2, row_t2, index, gain, sib_index, sib_gain, sib_first, sib_t2):
    left, right = before_after(first[...], second[...])
    shape = (SLOTS, LANES)
    at_lane = lane(shape)
    row, col, weight = slots_of(first[...])
    row = row - jnp.where(odd_tile(), CX - 2, 0)
    sib_index[...] = (at_lane - col + L_ROOM) & (LANES - 1)
    touched = (at_lane >= col) & (at_lane < col + R) & (row >= 0) & (row < 2)
    sib_gain[...] = jnp.where(touched, area_ratio * weight, 0.0)
    sib_first[...] = jnp.where(jnp.broadcast_to(row, shape) == 0, 1.0, 0.0)
    chosen = jnp.where((at_lane == row) & (row < 2), 1.0, 0.0)
    turned_8 = jnp.transpose(chosen)[0:16]
    sib_t2[...] = jnp.concatenate([turned_8, turned_8], 1).astype(bf16)
    turned = []
    for part, side in enumerate((right, left)):
        rows = slice(part * SLOTS, (part + 1) * SLOTS)
        row, col, weight = slots_of(side)
        chosen = jnp.where(at_lane == row, 1.0, 0.0)
        row2[rows] = (chosen + roll(chosen, CX)).astype(bf16)
        turned.append(jnp.transpose(chosen)[0:CX].astype(bf16))
        if part == 0:
            touched = (at_lane < 2) & (at_lane >= col)
            index[rows] = (at_lane - col + L_NEAR) & (LANES - 1)
        else:
            touched = (at_lane >= LANES - 2) & (at_lane < col + R)
            index[rows] = (at_lane - col + (L_NEAR + 2 - 30)) & (LANES - 1)
        gain[rows] = jnp.where(touched, area_ratio * weight, 0.0)
    row_t2[...] = jnp.concatenate(turned + turned, 1)


def before_after(first, second):
    odd = odd_tile()
    return jnp.where(odd, first, second), jnp.where(odd, second, first)


def gate(there, cells):
    return jnp.where(there, cells, 0.0)


def send_kernel(step, *refs):
    tile, district = lax.axis_index("tile"), lax.axis_index("district")
    has_left, has_right = tile > 0, tile < TILES - 1
    has_above, has_below = district > 0, district < lax.axis_size("district") - 1
    last = step == STEPS - 1
    if step == 0:
        (
            place, parent, parent_depth, child, child_depth, child_wet, above0, below0, cols0, cols1, reply, row2, index_s,
            eta_o, u_o, v_o, peta_o, pu_o, pv_o, street_o, out, *more, eta_x, flux_x, u_x, peta_x, pflux_x, pu_x,
        ) = refs
        u_x[8 : 8 + CX] = child[1]
        u_x[7:8] = gate(has_above, above0[2:3])
        u_x[8 + CX : 9 + CX] = gate(has_below, below0[2:3])
        pu_x[8 : 8 + PX] = parent[1]
        pu_x[7:8] = gate(has_above, above0[9:10])
        pu_x[8 + PX : 9 + PX] = gate(has_below, below0[9:10])
        eta_x[8 : 8 + CX] = child[0]
        peta_x[8 : 8 + PX] = parent[0]
        eta_x[6:8] = gate(has_above, above0[0:2])
        eta_x[8 + CX : 10 + CX] = gate(has_below, below0[0:2])
        peta_x[6:8] = gate(has_above, above0[7:9])
        peta_x[8 + PX : 10 + PX] = gate(has_below, below0[7:9])
        left, right = before_after(cols0[0:8], cols1[0:8])
        left, right = gate(has_left, left), gate(has_right, right)
        v, v_h = child[2], unpack2(left, right, 32, 8)
        eta_h = unpack4(left, right, 0, 8)
        pv, pv_h = parent[2], unpack2(left, right, 120, 2)
        peta_h = unpack4(left, right, 112, 2)
    else:
        (
            place, parent_depth, child_depth, child_wet, above0, below0, cols0, cols1, reply, row2, index_s,
            moved, swapped, eta_i, u_x, v_i, vh_i, etah_i, peta_i, pu_x, pv_i, pvh_i, petah_i,
            eta_o, u_o, v_o, peta_o, pu_o, pv_o, street_o, out, *more, eta_x, flux_x, peta_x, pflux_x,
        ) = refs
        mine, other = moved[0:4], swapped[4:8]
        above, below = jnp.where(odd_tile(), mine, other), jnp.where(odd_tile(), other, mine)
        eta_x[8 : 8 + CX] = eta_i[...]
        peta_x[8 : 8 + PX] = peta_i[...]
        eta_x[6:8] = gate(has_above, above[0:2])
        eta_x[8 + CX : 10 + CX] = gate(has_below, below[0:2])
        peta_x[6:8] = gate(has_above, above[2:4])
        peta_x[8 + PX : 10 + PX] = gate(has_below, below[2:4])
        left, right = before_after(cols0[0:8], cols1[0:8])
        left, right = gate(has_left, left), gate(has_right, right)
        v, v_h, eta_h = v_i[...], vh_i[...], etah_i[...]
        pv, pv_h, peta_h = pv_i[...], pvh_i[...], petah_i[...]
    wet = child_wet[step].astype(f32)
    q = child_depth[...] * wet
    q_up = gate(has_above, above0[3 + step : 4 + step])
    q_dn = gate(has_below, below0[3 + step : 4 + step])
    pq_up, pq_dn = gate(has_above, above0[10:11]), gate(has_below, below0[10:11])
    q_h = unpack2(left, right, 48 + 16 * step, 8)
    eta, u, u_up, u_dn, v, v_h = advance(eta_x, u_x, v, v_h, eta_h, q, q_up, q_dn, q_h, flux_x, CX)
    street = pick(row2[...], eta)
    peta, pu, pu_up, pu_dn, pv, pv_h = advance(
        peta_x, pu_x, pv, pv_h, peta_h, parent_depth[...], pq_up, pq_dn, unpack2(left, right, 124, 2), pflux_x, PX
    )
    eta_o[...] = eta
    u_o[8 : 8 + CX] = wet * u
    v_o[...] = wet * v
    peta_o[...] = peta
    pu_o[8 : 8 + PX] = pu
    pv_o[...] = pv
    street_o[...] = street
    if not last:
        vh_o, pvh_o = more
        u_o[7:8] = wet_of(q_up) * u_up
        u_o[8 + CX : 9 + CX] = wet_of(q_dn) * u_dn
        vh_o[...] = wet_of(q_h) * v_h
        pu_o[7:8] = pu_up
        pu_o[8 + PX : 9 + PX] = pu_dn
        pvh_o[...] = pv_h
    shape = (8, LANES)
    at_lane = lane(shape)
    common = pack4(jnp.zeros(shape, f32), eta, L_CCOL)
    common = pack4(common, peta, L_PCOL)
    first_row, first_col = place[0:8], place[8:16]
    lines = []
    for k in range(2):
        halves_of = [jnp.where(sub(shape) + g == first_row + k, peta[g : g + 8], 0.0) for g in (0, 8)]
        lines.append(jnp.sum(halves_of[0] + halves_of[1], axis=0, keepdims=True))
    lines = jnp.where(sub(shape) < 4, lines[0], lines[1])
    index = first_col - LANES * tile + 4 * (at_lane - L_WIN) + (sub(shape) & 3)
    window = along(lines, index & (LANES - 1))
    window = jnp.where((index >= 0) & (index < LANES), window, 0.0)
    common = jnp.where((at_lane >= L_WIN) & (at_lane < L_CCOL), window, common)
    street = along(street, index_s[...])
    if not last:
        odd = odd_tile()
        rest = pack_rows(jnp.zeros(shape, f32), jnp.where(odd, eta[0:2], eta[CX - 2 : CX]), L_CROW)
        rest = pack_rows(rest, jnp.where(odd, peta[0:2], peta[PX - 2 : PX]), L_PROW)
    for t in range(TILES):
        rows = slice(t * CAP, (t + 1) * CAP)
        out[t, 0:CAP] = jnp.where(at_lane < R, street[rows], jnp.where(at_lane < L_PCOL, reply[rows], common))
        if not last:
            rows = slice((t ^ 1) * CAP, ((t ^ 1) + 1) * CAP)
            out[t, CAP : 2 * CAP] = jnp.where(at_lane < L_NEAR, reply[rows], rest)


def windows_sum(inbox):
    parts = [inbox[8 * t : 8 * t + 8] for t in range(TILES)]
    while len(parts) > 1:
        parts = [parts[i] + parts[i + 1] for i in range(0, len(parts), 2)]
    return parts[0]


def nudge(eta, target):
    return eta + nudging * (target - eta)


def street_update(inbox, eta, street, row_t2, index_a, gain, lower):
    shape = (8, LANES)
    windows = windows_sum(inbox)
    mine = along(windows, jnp.full(shape, L_WIN, i32) + lax.axis_index("tile"))
    mine = jnp.where((sub(shape) & 3) == lane(shape) // R, mine, 0.0)
    target0 = jnp.sum(mine[0:4], axis=0, keepdims=True)
    target1 = jnp.sum(mine[4:8], axis=0, keepdims=True)
    eta = jnp.concatenate([nudge(eta[0:R], target0), nudge(eta[R:CX], target1)], 0)
    levels = nudge(street, jnp.where(lower > 0, target1, target0))
    flow = gain * (4.0 * levels - along(inbox, index_a))
    return eta - pick(row_t2, flow), windows


def room_flow(inbox, windows, face):
    shape = (SLOTS, LANES)
    at_lane = lane(shape)
    holder = jnp.where(at_lane == L_WIN + sub(shape) // CAP, 1.0, 0.0).astype(bf16)
    high = windows.astype(bf16)
    low = (windows - high.astype(f32)).astype(bf16)
    per_slot = lax.dot_general(
        jnp.concatenate([holder, holder], 1),
        jnp.concatenate([jnp.concatenate([high, low], 1), jnp.zeros((LANES - 8, 2 * LANES), bf16)], 0),
        (((1,), (1,)), ((), ())),
        preferred_element_type=f32,
    )
    weight = inbox[:, L_FIX : L_FIX + 1]
    col = inbox[:, L_FIX + 1 : L_FIX + 2].astype(i32)
    half = inbox[:, L_FIX + 2 : L_FIX + 3].astype(i32)
    cell = at_lane // 4
    target = along(per_slot, 4 * half + ((col + cell) // R & 3))
    levels = nudge(along(inbox, cell), target)
    return weight * (levels - face)


def street_kernel(
    inbox, eta, street, row_t2, index_a, gain, lower, peta, sib_index, sib_gain, sib_first, sib_t2, eta_o, message, windows_o
):
    eta, windows = street_update(
        for_me(inbox), eta[...], street[...], row_t2[...], index_a[...], gain[...], lower[...]
    )
    eta_o[...] = eta
    windows_o[...] = windows
    odd = odd_tile()
    shape = (8, LANES)
    packed = inbox[sibling(), CAP : 2 * CAP]
    row0, row1 = unpack_rows(packed, L_CROW)
    prow0, prow1 = unpack_rows(packed, L_PROW)
    target = along(windows, jnp.full(shape, L_WIN, i32) + sibling())
    target = jnp.where((sub(shape) & 3) == lane(shape) // R, target, 0.0)
    target = jnp.sum(jnp.where(odd, target[4:8], target[0:4]), axis=0, keepdims=True)
    row0, row1 = nudge(row0, target), nudge(row1, target)
    levels = jnp.where(sib_first[...] > 0, row0, row1)
    sums = along(inbox[:, CAP : 2 * CAP].reshape(SLOTS, LANES), sib_index[...])
    lost = pick(sib_t2[...], sib_gain[...] * (4.0 * levels - sums))
    message[0:2] = jnp.where(odd, eta[CX - 2 : CX], eta[0:2])
    message[2:4] = jnp.where(odd, peta[PX - 2 : PX], peta[0:2])
    message[4:5] = row0 - lost[0:1]
    message[5:6] = row1 - lost[1:2]
    message[6:7] = prow0
    message[7:8] = prow1


def room_kernel(
    step, inbox, windows, room, room_wet, face, door2, door_t2, fixed, near2, near_t2, near_index, near_gain,
    room_new, face_o, reply, etah_o, petah_o, eta_x, flux_x,
):
    received = for_me(inbox)
    flow = room_flow(received, windows[...], face[...])
    eta = room[0] + pick(door_t2[...], flow)
    eta, u, v = room_advance(eta, room[1], room[2], room_wet[step].astype(f32), eta_x, flux_x)
    room_new[0] = eta
    room_new[1] = u
    room_new[2] = v
    face_o[...], reply[...] = room_reply(eta, door2[...], fixed[...])
    tile = lax.axis_index("tile")
    left = inbox[lax.rem(tile + TILES - 1, TILES), 0:CAP]
    right = inbox[lax.rem(tile + 1, TILES), 0:CAP]
    at_lane = lane((8, LANES))

    def kept(cells):
        return jnp.where(jnp.where(lane(cells.shape) < R, TILES - 1 - tile, tile) > 0, cells, 0.0)

    petah_o[...] = kept(unpack4(left, right, L_PCOL, 2))
    eta_h = unpack4(left, right, L_CCOL, 8)
    spread = along(windows[...], L_WIN + ((jnp.where(at_lane < R, tile + 1, tile - 1)) & (TILES - 1)))
    target0 = jnp.where(at_lane < R, spread[0:1], spread[3:4])
    target1 = jnp.where(at_lane < R, spread[4:5], spread[7:8])
    eta_h = nudge(eta_h, jnp.concatenate([target0] * 4 + [target1] * 4, 0))
    levels = pick(near2[...], eta_h)
    sums = along(jnp.concatenate([received, received], 0), near_index[...])
    eta_h = eta_h - pick(near_t2[...], near_gain[...] * (4.0 * levels - sums))
    etah_o[...] = kept(eta_h)


def final_kernel(
    inbox, eta, street, row_t2, index_a, gain, lower, u_x, v, peta, pu_x, pv, room, face, door_t2,
    parent_o, child_o, room_o, child_eta, room_eta, done,
):
    pairs = [
        (u_x.at[pl.ds(8, CX)], child_o.at[1]), (v, child_o.at[2]), (peta, parent_o.at[0]),
        (pu_x.at[pl.ds(8, PX)], parent_o.at[1]), (pv, parent_o.at[2]), (room.at[1], room_o.at[1]),
        (room.at[2], room_o.at[2]), (room_eta, room_o.at[0]), (child_eta, child_o.at[0]),
    ]
    copies = [pltpu.make_async_copy(src, dst, done.at[k]) for k, (src, dst) in enumerate(pairs)]
    for copy in copies[:-2]:
        copy.start()
    received = for_me(inbox)
    child_eta[...], windows = street_update(
        received, eta[...], street[...], row_t2[...], index_a[...], gain[...], lower[...]
    )
    copies[-1].start()
    room_eta[...] = room[0] + pick(door_t2[...], room_flow(received, windows, face[...]))
    copies[-2].start()
    for copy in copies:
        copy.wait()


def sds(*shape, dtype=f32):
    return jax.ShapeDtypeStruct(shape, dtype)


VMEM = pl.BlockSpec(memory_space=pltpu.VMEM)
HBM = pl.BlockSpec(memory_space=pltpu.HBM)


def call(name, kernel, outs, args, scratch=(), us=1, reads=VMEM, writes=VMEM, limit=16):
    return pl.pallas_call(
        kernel,
        out_shape=outs,
        in_specs=[reads] * len(args),
        out_specs=[writes] * len(outs),
        scratch_shapes=[pltpu.VMEM((rows, LANES), f32) if isinstance(rows, int) else rows for rows in scratch],
        compiler_params=pltpu.CompilerParams(vmem_limit_bytes=limit * 2**20),
        cost_estimate=pl.CostEstimate(flops=1000000 * us, bytes_accessed=1000000 * us, transcendentals=0),
        name=name,
    )(*args)


def to_next(cells, axis):
    count = lax.axis_size(axis)
    return lax.ppermute(cells, axis, [(i, (i + 1) % count) for i in range(count)])


def to_previous(cells, axis):
    count = lax.axis_size(axis)
    return lax.ppermute(cells, axis, [((i + 1) % count, i) for i in range(count)])


def snake(cells):
    districts, tiles = lax.axis_size("district"), lax.axis_size("tile")
    pairs = []
    for d in range(districts):
        for t in range(tiles):
            to = d + 1 if t % 2 else d - 1
            target = (to, t) if 0 <= to < districts else (d, t ^ 1)
            pairs.append((d * tiles + t, target[0] * tiles + target[1]))
    return lax.ppermute(cells, ("district", "tile"), pairs)


def swap(cells, axis, which):
    count = lax.axis_size(axis)
    partner = [i + 1 if i % 2 == which else i - 1 for i in range(count)]
    return lax.ppermute(cells, axis, [(i, p if 0 <= p < count else i) for i, p in enumerate(partner)])


def body(
    parent_state,
    parent_depth,
    child_state,
    child_depth,
    child_wet,
    interior_state,
    interior_wet,
    parent_anchor,
    open_row,
    open_col,
    open_owner,
    open_valid,
    open_conduct,
    door_rows,
):
    block, tall = sds(CX, LANES), sds(CX + 16, LANES)
    pblock, ptall = sds(PX, LANES), sds(PX + 16, LANES)
    grid, tile8, tile16 = sds(SLOTS, LANES), sds(8, LANES), sds(16, LANES)
    rooms = sds(3, CX, LANES)

    def flat(values):
        return values.reshape(1, -1)

    openings = [flat(open_row), flat(open_col), flat(open_owner), flat(open_valid), flat(open_conduct)]
    inputs = [parent_state, parent_depth, child_state, child_depth, child_wet, *openings]
    up, dn, side = call(
        "edges",
        edges_kernel,
        [tile16] * 3,
        inputs,
        scratch=[pltpu.VMEM(a.shape, a.dtype) for a in inputs] + [pltpu.SemaphoreType.DMA((16,))],
        reads=HBM,
        limit=60,
    )
    cols0, cols1 = swap(side, "tile", 0), swap(side, "tile", 1)
    row2, row_t2, index_s, index_a, gain, lower, fixed, door2, door_t2, room, face, reply, place = call(
        "setup",
        setup_kernel,
        [
            sds(SLOTS, LANES, dtype=bf16), sds(CX, 2 * SLOTS, dtype=bf16), sds(SLOTS, LANES, dtype=i32),
            sds(SLOTS, LANES, dtype=i32), grid, grid, grid, sds(SLOTS, LANES, dtype=bf16),
            sds(CX, 2 * SLOTS, dtype=bf16), rooms, grid, grid, sds(16, LANES, dtype=i32),
        ],
        [*openings, jnp.transpose(parent_anchor, (0, 2, 1))[0], door_rows, interior_state, interior_wet],
        scratch=(CX + 16, CX + 16, 16),
    )
    above0 = to_next(dn, "district")
    below0 = to_previous(up, "district")
    near = call(
        "near",
        near_kernel,
        [
            sds(2 * SLOTS, LANES, dtype=bf16), sds(CX, 4 * SLOTS, dtype=bf16), sds(2 * SLOTS, LANES, dtype=i32),
            sds(2 * SLOTS, LANES), sds(SLOTS, LANES, dtype=i32), grid, grid, sds(16, 2 * SLOTS, dtype=bf16),
        ],
        [cols0, cols1],
    )
    near, siblings = near[:4], near[4:]
    for step in range(STEPS):
        with_step = lambda *refs, step=step: send_kernel(step, *refs)
        if step == 0:
            args = [
                place, parent_state, parent_depth, child_state, child_depth, child_wet, above0, below0, cols0, cols1,
                reply, row2, index_s,
            ]
            scratch = (CX + 16,) * 3 + (PX + 16,) * 3
        else:
            args = [
                place, parent_depth, child_depth, child_wet, above0, below0, cols0, cols1, reply, row2, index_s,
                moved, swapped, eta, u, v, v_h, eta_h, peta, pu, pv, pv_h, peta_h,
            ]
            scratch = (CX + 16,) * 2 + (PX + 16,) * 2
        outs = [block, tall, block, pblock, ptall, pblock, grid, sds(TILES, CAP if step == STEPS - 1 else 2 * CAP, LANES)]
        if step < STEPS - 1:
            outs += [block, pblock]
        eta, u, v, peta, pu, pv, street, outbox, *more = call(f"send{step}", with_step, outs, args, scratch=scratch)
        inbox = lax.all_to_all(outbox, "tile", split_axis=0, concat_axis=0, tiled=True)
        shared = [inbox, eta, street, row_t2, index_a, gain, lower]
        if step == STEPS - 1:
            return tuple(
                call(
                    "final",
                    final_kernel,
                    [sds(3, PX, LANES), rooms, rooms],
                    shared + [u, v, peta, pu, pv, room, face, door_t2],
                    scratch=(CX, CX, pltpu.SemaphoreType.DMA((9,))),
                    writes=HBM,
                )
            )
        v_h, pv_h = more
        eta, message, windows = call(
            f"street{step}", street_kernel, [block, tile8, tile8], [*shared, peta, *siblings]
        )
        moved = snake(message)
        with_step = lambda *refs, step=step: room_kernel(step + 1, *refs)
        room, face, reply, eta_h, peta_h = call(
            f"room{step}",
            with_step,
            [rooms, grid, grid, block, pblock],
            [inbox, windows, room, interior_wet, face, door2, door_t2, fixed, *near],
            scratch=(CX + 16, CX + 16),
        )
        moved, reply = lax.optimization_barrier((moved, reply))
        swapped = swap(moved, "tile", 0)


def solution(mesh):
    return jax.shard_map(
        body,
        mesh=mesh,
        in_specs=(
            P(None, "district", "tile"),
            P("district", "tile"),
            P(None, "district", "tile"),
            P("district", "tile"),
            P(None, "district", "tile"),
            P(None, ("district", "tile"), None),
            P(None, ("district", "tile"), None),
            P("district", None, None),
            P(("district", "tile")),
            P(("district", "tile")),
            P(("district", "tile"), None),
            P(("district", "tile")),
            P(("district", "tile")),
            P(("district", "tile"), None),
        ),
        out_specs=(
            P(None, "district", "tile"),
            P(None, "district", "tile"),
            P(None, ("district", "tile"), None),
        ),
        check_vma=False,
    )
```

```python
import jax
import jax.numpy as jnp
from jax import lax
from jax.experimental import pallas as pl
from jax.experimental.pallas import tpu as pltpu
from jax.sharding import PartitionSpec as P

f32 = jnp.float32
bf16 = jnp.bfloat16
i32 = jnp.int32

CX = 64
PX = 16
LANES = 128
R = 32
STEPS = 4
CAP = 8
TILES = 16
SLOTS = TILES * CAP

courant = 0.3
nudging = 0.25
area_ratio = 0.0625

L_ROOM = 32
L_NEAR = 64
L_FIX = 68
L_PCOL = 72
L_WIN = 80
L_CCOL = 96
L_CROW = 64
L_PROW = 96


def lane(shape):
    return lax.broadcasted_iota(i32, shape, 1)


def sub(shape):
    return lax.broadcasted_iota(i32, shape, 0)


def roll(cells, by):
    return pltpu.roll(cells, by % LANES, 1)


def along(cells, index):
    return jnp.take_along_axis(cells, index, axis=1, mode="promise_in_bounds")


def halves(cells):
    high = cells.astype(bf16)
    low = (cells - high.astype(f32)).astype(bf16)
    return jnp.concatenate([high, low], 0)


def pick(selector, cells):
    return jnp.dot(selector, halves(cells), preferred_element_type=f32)


def pack4(packed, cells, at):
    at_lane = lane(packed.shape)
    for g in range(cells.shape[0] // 8):
        first = at + 4 * g
        moved = roll(cells[8 * g : 8 * g + 8], first + 2)
        packed = jnp.where((at_lane >= first) & (at_lane < first + 4), moved, packed)
    return packed


def pack2(packed, cells, at):
    at_lane = lane(packed.shape)
    for g in range(cells.shape[0] // 8):
        first = at + 2 * g
        moved = roll(cells[8 * g : 8 * g + 8], first + 1)
        packed = jnp.where((at_lane >= first) & (at_lane < first + 2), moved, packed)
    return packed


def unpack4(left, right, at, groups):
    chosen = jnp.where(lane(left.shape) % 4 >= 2, right, left)
    return jnp.concatenate([roll(chosen, -(at + 4 * g + 2)) for g in range(groups)], 0)


def unpack2(left, right, at, groups):
    chosen = jnp.where(lane(left.shape) % 2 == 1, right, left)
    return jnp.concatenate([roll(chosen, -(at + 2 * g + 1)) for g in range(groups)], 0)


def pack_rows(packed, rows, at):
    shape = packed.shape
    both = jnp.where(sub(shape) < 4, rows[0:1], rows[1:2])
    inside = (lane(shape) >= at) & (lane(shape) < at + R)
    for k in range(4):
        packed = jnp.where(inside & ((sub(shape) & 3) == k), roll(both, at - R * k), packed)
    return packed


def unpack_rows(packed, at):
    shape = packed.shape
    spread = jnp.zeros(shape, f32)
    for k in range(4):
        spread = jnp.where(((sub(shape) & 3) == k) & (lane(shape) // R == k), roll(packed, R * k - at), spread)
    return jnp.sum(spread[0:4], axis=0, keepdims=True), jnp.sum(spread[4:8], axis=0, keepdims=True)


def odd_tile():
    return lax.rem(lax.axis_index("tile"), 2) == 1


def sibling():
    tile = lax.axis_index("tile")
    return tile + 1 - 2 * lax.rem(tile, 2)


def for_me(inbox):
    return inbox[:, 0:CAP].reshape(SLOTS, LANES)


def advance(eta_x, u_x, v, v_h, eta_h, q, q_up, q_dn, q_h, flux_x, rows):
    top, end = 8, 8 + rows
    at_lane = lane((rows, LANES))
    first, last = at_lane == 0, at_lane == LANES - 1
    eta = eta_x[top:end]
    u_new = u_x[top:end] - courant * (eta_x[top + 1 : end + 1] - eta_x[top - 1 : end - 1])
    u_up = u_x[top - 1 : top] - courant * (eta_x[top : top + 1] - eta_x[top - 2 : top - 1])
    u_dn = u_x[end : end + 1] - courant * (eta_x[end + 1 : end + 2] - eta_x[end - 1 : end])
    after = roll(jnp.where(first, eta_h, eta), -1)
    before = roll(jnp.where(last, eta_h, eta), 1)
    v_new = v - courant * (after - before)
    after = roll(jnp.where(first, eta, eta_h), -1)
    before = roll(jnp.where(last, eta, eta_h), 1)
    v_edge = v_h - courant * (after - before)
    flux_x[top:end] = q * u_new
    flux_x[top - 1 : top] = q_up * u_up
    flux_x[end : end + 1] = q_dn * u_dn
    flux = q * v_new
    flux_h = q_h * v_edge
    after = roll(jnp.where(first, flux_h, flux), -1)
    before = roll(jnp.where(last, flux_h, flux), 1)
    eta_new = eta - courant * (
        flux_x[top + 1 : end + 1] - flux_x[top - 1 : end - 1] + after - before
    )
    return eta_new, u_new, u_up, u_dn, v_new, v_edge


def wet_of(q):
    return jnp.where(q > 0, 1.0, 0.0).astype(f32)


def room_advance(eta, u, v, wet, eta_x, flux_x):
    at_lane = lane((CX, LANES))
    first, last = at_lane == 0, at_lane == LANES - 1
    blank = jnp.zeros((8, LANES), f32)
    for ref in (eta_x, flux_x):
        ref[0:8] = blank
        ref[8 + CX : 16 + CX] = blank
    eta_x[8 : 8 + CX] = eta
    u_new = u - courant * (eta_x[9 : 9 + CX] - eta_x[7 : 7 + CX])
    v_new = v - courant * (
        jnp.where(last, 0.0, roll(eta, -1)) - jnp.where(first, 0.0, roll(eta, 1))
    )
    flux_x[8 : 8 + CX] = wet * u_new
    flux = wet * v_new
    eta_new = eta - courant * (
        flux_x[9 : 9 + CX]
        - flux_x[7 : 7 + CX]
        + jnp.where(last, 0.0, roll(flux, -1))
        - jnp.where(first, 0.0, roll(flux, 1))
    )
    return eta_new, wet * u_new, wet * v_new


def room_reply(eta, door2, fixed):
    sums = eta + roll(eta, -1)
    sums = sums + roll(sums, -2)
    at_lane = lane((CX, LANES))
    sums = along(sums, (4 * (at_lane - L_ROOM)) & (LANES - 1))
    both = pick(door2, jnp.concatenate([eta, sums], 1))
    rows, sums = both[:, :LANES], both[:, LANES:]
    ahead = roll(jnp.concatenate([sums[8:], sums[:8]], 0), L_NEAR - L_ROOM)
    behind = roll(jnp.concatenate([sums[-8:], sums[:-8]], 0), L_NEAR + 2 - (L_ROOM + 30))
    at_lane = lane(sums.shape)
    reply = jnp.where(
        at_lane < L_NEAR,
        sums,
        jnp.where(at_lane < L_NEAR + 2, ahead, jnp.where(at_lane < L_FIX, behind, fixed)),
    )
    return rows, reply


def slots_of(side):
    shape = (SLOTS, LANES)
    owner = jnp.broadcast_to(side[8:9], shape)
    earlier = (jnp.transpose(owner) == owner) & (sub(shape) < lane(shape))
    rank = jnp.sum(jnp.where(earlier, 1.0, 0.0), axis=0, keepdims=True)
    held = sub(shape).astype(f32) == jnp.where(side[8:9] >= 0, side[8:9] * CAP + rank, -1.0)

    def take(values):
        return jnp.sum(jnp.where(held, values, 0.0), axis=1, keepdims=True)

    row = take(side[9:10] + 1.0) - 1.0
    return row.astype(i32), take(side[10:11]).astype(i32), take(side[11:12])


def list_openings(side, row, col, owner, valid, conduct):
    count = owner.shape[1]
    side[8:9] = jnp.full((1, LANES), -1.0, f32)
    side[8:9, 0:count] = owner[...].astype(f32)
    side[9:10, 0:count] = row[...].astype(f32)
    side[10:11, 0:count] = col[...].astype(f32)
    side[11:12, 0:count] = conduct[...] * valid[...].astype(f32)


def edges_kernel(
    parent_i, parent_depth_i, child_i, child_depth_i, child_wet_i, row_i, col_i, owner_i, valid_i, conduct_i,
    up, dn, side,
    parent, parent_depth, child, child_depth, child_wet, row, col, owner, valid, conduct, done,
):
    pairs = [(child_wet_i.at[s], child_wet.at[s]) for s in range(STEPS)]
    pairs += [(child_i.at[f], child.at[f]) for f in (0, 2)]
    pairs += [(child_i.at[1, pl.ds(r, 8)], child.at[1, pl.ds(r, 8)]) for r in (0, CX - 8)]
    pairs += [
        (child_depth_i, child_depth), (parent_i, parent), (parent_depth_i, parent_depth),
        (row_i, row), (col_i, col), (owner_i, owner), (valid_i, valid), (conduct_i, conduct),
    ]
    copies = [pltpu.make_async_copy(src, dst, done.at[k]) for k, (src, dst) in enumerate(pairs)]
    for copy in copies:
        copy.start()
    up[...] = jnp.zeros((16, LANES), f32)
    dn[...] = jnp.zeros((16, LANES), f32)
    side[...] = jnp.zeros((16, LANES), f32)
    for copy in copies:
        copy.wait()
    eta = child[0]
    packed = pack4(jnp.zeros((8, LANES), f32), eta, 0)
    packed = pack2(packed, child[2], 32)
    up[0:2] = eta[0:2]
    dn[0:2] = eta[CX - 2 : CX]
    up[2:3] = child[1, 0:1]
    dn[2:3] = child[1, CX - 1 : CX]
    for s in range(STEPS):
        q = child_depth[...] * child_wet[s].astype(f32)
        up[3 + s : 4 + s] = q[0:1]
        dn[3 + s : 4 + s] = q[CX - 1 : CX]
        packed = pack2(packed, q, 48 + 16 * s)
    eta = parent[0]
    up[7:9] = eta[0:2]
    dn[7:9] = eta[PX - 2 : PX]
    up[9:10] = parent[1, 0:1]
    dn[9:10] = parent[1, PX - 1 : PX]
    up[10:11] = parent_depth[0:1]
    dn[10:11] = parent_depth[PX - 1 : PX]
    packed = pack4(packed, eta, 112)
    packed = pack2(packed, parent[2], 120)
    packed = pack2(packed, parent_depth[...], 124)
    side[0:8] = packed
    list_openings(side, row, col, owner, valid, conduct)


def setup_kernel(
    opening_row, opening_col, owner, valid, conduct, anchor, door, room, room_wet, row2, row_t2, index_s, index_a, gain, lower, fixed,
    door2, door_t2, room_new, face, reply, place, eta_x, flux_x, side,
):
    side[8:16] = jnp.zeros((8, LANES), f32)
    list_openings(side, opening_row, opening_col, owner, valid, conduct)
    place[0:8] = jnp.broadcast_to(anchor[0:1, 0:1], (8, LANES))
    place[8:16] = jnp.broadcast_to(anchor[1:2, 0:1], (8, LANES))
    shape = (SLOTS, LANES)
    at_lane = lane(shape)
    row, col, weight = slots_of(side[...])
    chosen = jnp.where(at_lane == row, 1.0, 0.0)
    row2[...] = (chosen + roll(chosen, CX)).astype(bf16)
    turned = jnp.transpose(chosen)[0:CX].astype(bf16)
    row_t2[...] = jnp.concatenate([turned, turned], 1)
    index_s[...] = (at_lane + col) & (LANES - 1)
    index_a[...] = (at_lane - col + L_ROOM) & (LANES - 1)
    inside = (at_lane >= col) & (at_lane < col + R)
    gain[...] = jnp.where(inside, area_ratio * weight, 0.0)
    half = jnp.where(row >= R, 1.0, 0.0)
    lower[...] = jnp.broadcast_to(half, shape)
    fixed_now = jnp.where(
        at_lane == L_FIX,
        weight,
        jnp.where(at_lane == L_FIX + 1, col.astype(f32), jnp.where(at_lane == L_FIX + 2, half, 0.0)),
    )
    fixed[...] = fixed_now
    chosen_t = jnp.where(sub(shape) == door[...], 1.0, 0.0)
    turned = chosen_t[0:CX].astype(bf16)
    door_t2[...] = jnp.concatenate([turned, turned], 1)
    chosen = jnp.transpose(chosen_t)
    both = (chosen + roll(chosen, CX)).astype(bf16)
    door2[...] = both
    eta, u, v = room_advance(room[0], room[1], room[2], room_wet[0].astype(f32), eta_x, flux_x)
    room_new[0] = eta
    room_new[1] = u
    room_new[2] = v
    face[...], reply[...] = room_reply(eta, both, fixed_now)


def near_kernel(first, second, row2, row_t2, index, gain, sib_index, sib_gain, sib_first, sib_t2):
    left, right = before_after(first[...], second[...])
    shape = (SLOTS, LANES)
    at_lane = lane(shape)
    row, col, weight = slots_of(first[...])
    row = row - jnp.where(odd_tile(), CX - 2, 0)
    sib_index[...] = (at_lane - col + L_ROOM) & (LANES - 1)
    touched = (at_lane >= col) & (at_lane < col + R) & (row >= 0) & (row < 2)
    sib_gain[...] = jnp.where(touched, area_ratio * weight, 0.0)
    sib_first[...] = jnp.where(jnp.broadcast_to(row, shape) == 0, 1.0, 0.0)
    chosen = jnp.where((at_lane == row) & (row < 2), 1.0, 0.0)
    turned_8 = jnp.transpose(chosen)[0:16]
    sib_t2[...] = jnp.concatenate([turned_8, turned_8], 1).astype(bf16)
    turned = []
    for part, side in enumerate((right, left)):
        rows = slice(part * SLOTS, (part + 1) * SLOTS)
        row, col, weight = slots_of(side)
        chosen = jnp.where(at_lane == row, 1.0, 0.0)
        row2[rows] = (chosen + roll(chosen, CX)).astype(bf16)
        turned.append(jnp.transpose(chosen)[0:CX].astype(bf16))
        if part == 0:
            touched = (at_lane < 2) & (at_lane >= col)
            index[rows] = (at_lane - col + L_NEAR) & (LANES - 1)
        else:
            touched = (at_lane >= LANES - 2) & (at_lane < col + R)
            index[rows] = (at_lane - col + (L_NEAR + 2 - 30)) & (LANES - 1)
        gain[rows] = jnp.where(touched, area_ratio * weight, 0.0)
    row_t2[...] = jnp.concatenate(turned + turned, 1)


def before_after(first, second):
    odd = odd_tile()
    return jnp.where(odd, first, second), jnp.where(odd, second, first)


def gate(there, cells):
    return jnp.where(there, cells, 0.0)


def send_kernel(step, *refs):
    tile, district = lax.axis_index("tile"), lax.axis_index("district")
    has_left, has_right = tile > 0, tile < TILES - 1
    has_above, has_below = district > 0, district < lax.axis_size("district") - 1
    last = step == STEPS - 1
    if step == 0:
        (
            place, parent, parent_depth, child, child_depth, child_wet, above0, below0, cols0, cols1, reply, row2, index_s,
            eta_o, u_o, v_o, peta_o, pu_o, pv_o, street_o, out, *more, eta_x, flux_x, u_x, peta_x, pflux_x, pu_x,
        ) = refs
        u_x[8 : 8 + CX] = child[1]
        u_x[7:8] = gate(has_above, above0[2:3])
        u_x[8 + CX : 9 + CX] = gate(has_below, below0[2:3])
        pu_x[8 : 8 + PX] = parent[1]
        pu_x[7:8] = gate(has_above, above0[9:10])
        pu_x[8 + PX : 9 + PX] = gate(has_below, below0[9:10])
        eta_x[8 : 8 + CX] = child[0]
        peta_x[8 : 8 + PX] = parent[0]
        eta_x[6:8] = gate(has_above, above0[0:2])
        eta_x[8 + CX : 10 + CX] = gate(has_below, below0[0:2])
        peta_x[6:8] = gate(has_above, above0[7:9])
        peta_x[8 + PX : 10 + PX] = gate(has_below, below0[7:9])
        left, right = before_after(cols0[0:8], cols1[0:8])
        left, right = gate(has_left, left), gate(has_right, right)
        v, v_h = child[2], unpack2(left, right, 32, 8)
        eta_h = unpack4(left, right, 0, 8)
        pv, pv_h = parent[2], unpack2(left, right, 120, 2)
        peta_h = unpack4(left, right, 112, 2)
    else:
        (
            place, parent_depth, child_depth, child_wet, above0, below0, cols0, cols1, reply, row2, index_s,
            moved, swapped, eta_i, u_x, v_i, vh_i, etah_i, peta_i, pu_x, pv_i, pvh_i, petah_i,
            eta_o, u_o, v_o, peta_o, pu_o, pv_o, street_o, out, *more, eta_x, flux_x, peta_x, pflux_x,
        ) = refs
        mine, other = moved[0:4], swapped[4:8]
        above, below = jnp.where(odd_tile(), mine, other), jnp.where(odd_tile(), other, mine)
        eta_x[8 : 8 + CX] = eta_i[...]
        peta_x[8 : 8 + PX] = peta_i[...]
        eta_x[6:8] = gate(has_above, above[0:2])
        eta_x[8 + CX : 10 + CX] = gate(has_below, below[0:2])
        peta_x[6:8] = gate(has_above, above[2:4])
        peta_x[8 + PX : 10 + PX] = gate(has_below, below[2:4])
        left, right = before_after(cols0[0:8], cols1[0:8])
        left, right = gate(has_left, left), gate(has_right, right)
        v, v_h, eta_h = v_i[...], vh_i[...], etah_i[...]
        pv, pv_h, peta_h = pv_i[...], pvh_i[...], petah_i[...]
    wet = child_wet[step].astype(f32)
    q = child_depth[...] * wet
    q_up = gate(has_above, above0[3 + step : 4 + step])
    q_dn = gate(has_below, below0[3 + step : 4 + step])
    pq_up, pq_dn = gate(has_above, above0[10:11]), gate(has_below, below0[10:11])
    q_h = unpack2(left, right, 48 + 16 * step, 8)
    eta, u, u_up, u_dn, v, v_h = advance(eta_x, u_x, v, v_h, eta_h, q, q_up, q_dn, q_h, flux_x, CX)
    street = pick(row2[...], eta)
    peta, pu, pu_up, pu_dn, pv, pv_h = advance(
        peta_x, pu_x, pv, pv_h, peta_h, parent_depth[...], pq_up, pq_dn, unpack2(left, right, 124, 2), pflux_x, PX
    )
    eta_o[...] = eta
    u_o[8 : 8 + CX] = wet * u
    v_o[...] = wet * v
    peta_o[...] = peta
    pu_o[8 : 8 + PX] = pu
    pv_o[...] = pv
    street_o[...] = street
    if not last:
        vh_o, pvh_o = more
        u_o[7:8] = wet_of(q_up) * u_up
        u_o[8 + CX : 9 + CX] = wet_of(q_dn) * u_dn
        vh_o[...] = wet_of(q_h) * v_h
        pu_o[7:8] = pu_up
        pu_o[8 + PX : 9 + PX] = pu_dn
        pvh_o[...] = pv_h
    shape = (8, LANES)
    at_lane = lane(shape)
    common = pack4(jnp.zeros(shape, f32), eta, L_CCOL)
    common = pack4(common, peta, L_PCOL)
    first_row, first_col = place[0:8], place[8:16]
    lines = []
    for k in range(2):
        halves_of = [jnp.where(sub(shape) + g == first_row + k, peta[g : g + 8], 0.0) for g in (0, 8)]
        lines.append(jnp.sum(halves_of[0] + halves_of[1], axis=0, keepdims=True))
    lines = jnp.where(sub(shape) < 4, lines[0], lines[1])
    index = first_col - LANES * tile + 4 * (at_lane - L_WIN) + (sub(shape) & 3)
    window = along(lines, index & (LANES - 1))
    window = jnp.where((index >= 0) & (index < LANES), window, 0.0)
    common = jnp.where((at_lane >= L_WIN) & (at_lane < L_CCOL), window, common)
    street = along(street, index_s[...])
    if not last:
        odd = odd_tile()
        rest = pack_rows(jnp.zeros(shape, f32), jnp.where(odd, eta[0:2], eta[CX - 2 : CX]), L_CROW)
        rest = pack_rows(rest, jnp.where(odd, peta[0:2], peta[PX - 2 : PX]), L_PROW)
    for t in range(TILES):
        rows = slice(t * CAP, (t + 1) * CAP)
        out[t, 0:CAP] = jnp.where(at_lane < R, street[rows], jnp.where(at_lane < L_PCOL, reply[rows], common))
        if not last:
            rows = slice((t ^ 1) * CAP, ((t ^ 1) + 1) * CAP)
            out[t, CAP : 2 * CAP] = jnp.where(at_lane < L_NEAR, reply[rows], rest)


def windows_sum(inbox):
    parts = [inbox[8 * t : 8 * t + 8] for t in range(TILES)]
    while len(parts) > 1:
        parts = [parts[i] + parts[i + 1] for i in range(0, len(parts), 2)]
    return parts[0]


def nudge(eta, target):
    return eta + nudging * (target - eta)


def street_update(inbox, eta, street, row_t2, index_a, gain, lower):
    shape = (8, LANES)
    windows = windows_sum(inbox)
    mine = along(windows, jnp.full(shape, L_WIN, i32) + lax.axis_index("tile"))
    mine = jnp.where((sub(shape) & 3) == lane(shape) // R, mine, 0.0)
    target0 = jnp.sum(mine[0:4], axis=0, keepdims=True)
    target1 = jnp.sum(mine[4:8], axis=0, keepdims=True)
    eta = jnp.concatenate([nudge(eta[0:R], target0), nudge(eta[R:CX], target1)], 0)
    levels = nudge(street, jnp.where(lower > 0, target1, target0))
    flow = gain * (4.0 * levels - along(inbox, index_a))
    return eta - pick(row_t2, flow), windows


def room_flow(inbox, windows, face):
    shape = (SLOTS, LANES)
    at_lane = lane(shape)
    holder = jnp.where(at_lane == L_WIN + sub(shape) // CAP, 1.0, 0.0).astype(bf16)
    high = windows.astype(bf16)
    low = (windows - high.astype(f32)).astype(bf16)
    per_slot = lax.dot_general(
        jnp.concatenate([holder, holder], 1),
        jnp.concatenate([jnp.concatenate([high, low], 1), jnp.zeros((LANES - 8, 2 * LANES), bf16)], 0),
        (((1,), (1,)), ((), ())),
        preferred_element_type=f32,
    )
    weight = inbox[:, L_FIX : L_FIX + 1]
    col = inbox[:, L_FIX + 1 : L_FIX + 2].astype(i32)
    half = inbox[:, L_FIX + 2 : L_FIX + 3].astype(i32)
    cell = at_lane // 4
    target = along(per_slot, 4 * half + ((col + cell) // R & 3))
    levels = nudge(along(inbox, cell), target)
    return weight * (levels - face)


def street_kernel(
    inbox, eta, street, row_t2, index_a, gain, lower, peta, sib_index, sib_gain, sib_first, sib_t2, eta_o, message, windows_o
):
    eta, windows = street_update(
        for_me(inbox), eta[...], street[...], row_t2[...], index_a[...], gain[...], lower[...]
    )
    eta_o[...] = eta
    windows_o[...] = windows
    odd = odd_tile()
    shape = (8, LANES)
    packed = inbox[sibling(), CAP : 2 * CAP]
    row0, row1 = unpack_rows(packed, L_CROW)
    prow0, prow1 = unpack_rows(packed, L_PROW)
    target = along(windows, jnp.full(shape, L_WIN, i32) + sibling())
    target = jnp.where((sub(shape) & 3) == lane(shape) // R, target, 0.0)
    target = jnp.sum(jnp.where(odd, target[4:8], target[0:4]), axis=0, keepdims=True)
    row0, row1 = nudge(row0, target), nudge(row1, target)
    levels = jnp.where(sib_first[...] > 0, row0, row1)
    sums = along(inbox[:, CAP : 2 * CAP].reshape(SLOTS, LANES), sib_index[...])
    lost = pick(sib_t2[...], sib_gain[...] * (4.0 * levels - sums))
    message[0:2] = jnp.where(odd, eta[CX - 2 : CX], eta[0:2])
    message[2:4] = jnp.where(odd, peta[PX - 2 : PX], peta[0:2])
    message[4:5] = row0 - lost[0:1]
    message[5:6] = row1 - lost[1:2]
    message[6:7] = prow0
    message[7:8] = prow1


def room_kernel(
    step, inbox, windows, room, room_wet, face, door2, door_t2, fixed, near2, near_t2, near_index, near_gain,
    room_new, face_o, reply, etah_o, petah_o, eta_x, flux_x,
):
    received = for_me(inbox)
    flow = room_flow(received, windows[...], face[...])
    eta = room[0] + pick(door_t2[...], flow)
    eta, u, v = room_advance(eta, room[1], room[2], room_wet[step].astype(f32), eta_x, flux_x)
    room_new[0] = eta
    room_new[1] = u
    room_new[2] = v
    face_o[...], reply[...] = room_reply(eta, door2[...], fixed[...])
    tile = lax.axis_index("tile")
    left = inbox[lax.rem(tile + TILES - 1, TILES), 0:CAP]
    right = inbox[lax.rem(tile + 1, TILES), 0:CAP]
    at_lane = lane((8, LANES))

    def kept(cells):
        return jnp.where(jnp.where(lane(cells.shape) < R, TILES - 1 - tile, tile) > 0, cells, 0.0)

    petah_o[...] = kept(unpack4(left, right, L_PCOL, 2))
    eta_h = unpack4(left, right, L_CCOL, 8)
    spread = along(windows[...], L_WIN + ((jnp.where(at_lane < R, tile + 1, tile - 1)) & (TILES - 1)))
    target0 = jnp.where(at_lane < R, spread[0:1], spread[3:4])
    target1 = jnp.where(at_lane < R, spread[4:5], spread[7:8])
    eta_h = nudge(eta_h, jnp.concatenate([target0] * 4 + [target1] * 4, 0))
    levels = pick(near2[...], eta_h)
    sums = along(jnp.concatenate([received, received], 0), near_index[...])
    eta_h = eta_h - pick(near_t2[...], near_gain[...] * (4.0 * levels - sums))
    etah_o[...] = kept(eta_h)


def final_kernel(
    inbox, eta, street, row_t2, index_a, gain, lower, u_x, v, peta, pu_x, pv, room, face, door_t2,
    parent_o, child_o, room_o, child_eta, room_eta, done,
):
    pairs = [
        (u_x.at[pl.ds(8, CX)], child_o.at[1]), (v, child_o.at[2]), (peta, parent_o.at[0]),
        (pu_x.at[pl.ds(8, PX)], parent_o.at[1]), (pv, parent_o.at[2]), (room.at[1], room_o.at[1]),
        (room.at[2], room_o.at[2]), (room_eta, room_o.at[0]), (child_eta, child_o.at[0]),
    ]
    copies = [pltpu.make_async_copy(src, dst, done.at[k]) for k, (src, dst) in enumerate(pairs)]
    for copy in copies[:-2]:
        copy.start()
    received = for_me(inbox)
    child_eta[...], windows = street_update(
        received, eta[...], street[...], row_t2[...], index_a[...], gain[...], lower[...]
    )
    copies[-1].start()
    room_eta[...] = room[0] + pick(door_t2[...], room_flow(received, windows, face[...]))
    copies[-2].start()
    for copy in copies:
        copy.wait()


def sds(*shape, dtype=f32):
    return jax.ShapeDtypeStruct(shape, dtype)


VMEM = pl.BlockSpec(memory_space=pltpu.VMEM)
HBM = pl.BlockSpec(memory_space=pltpu.HBM)


def call(name, kernel, outs, args, scratch=(), us=1, reads=VMEM, writes=VMEM, limit=16):
    return pl.pallas_call(
        kernel,
        out_shape=outs,
        in_specs=[reads] * len(args),
        out_specs=[writes] * len(outs),
        scratch_shapes=[pltpu.VMEM((rows, LANES), f32) if isinstance(rows, int) else rows for rows in scratch],
        compiler_params=pltpu.CompilerParams(vmem_limit_bytes=int(limit * 2**20)),
        cost_estimate=pl.CostEstimate(flops=1000000 * us, bytes_accessed=1000000 * us, transcendentals=0),
        name=name,
    )(*args)


def to_next(cells, axis):
    count = lax.axis_size(axis)
    return lax.ppermute(cells, axis, [(i, (i + 1) % count) for i in range(count)])


def to_previous(cells, axis):
    count = lax.axis_size(axis)
    return lax.ppermute(cells, axis, [((i + 1) % count, i) for i in range(count)])


def snake(cells):
    districts, tiles = lax.axis_size("district"), lax.axis_size("tile")
    pairs = []
    for d in range(districts):
        for t in range(tiles):
            to = d + 1 if t % 2 else d - 1
            target = (to, t) if 0 <= to < districts else (d, t ^ 1)
            pairs.append((d * tiles + t, target[0] * tiles + target[1]))
    return lax.ppermute(cells, ("district", "tile"), pairs)


def swap(cells, axis, which):
    count = lax.axis_size(axis)
    partner = [i + 1 if i % 2 == which else i - 1 for i in range(count)]
    return lax.ppermute(cells, axis, [(i, p if 0 <= p < count else i) for i, p in enumerate(partner)])


def body(
    parent_state,
    parent_depth,
    child_state,
    child_depth,
    child_wet,
    interior_state,
    interior_wet,
    parent_anchor,
    open_row,
    open_col,
    open_owner,
    open_valid,
    open_conduct,
    door_rows,
):
    block, tall = sds(CX, LANES), sds(CX + 16, LANES)
    pblock, ptall = sds(PX, LANES), sds(PX + 16, LANES)
    grid, tile8, tile16 = sds(SLOTS, LANES), sds(8, LANES), sds(16, LANES)
    rooms = sds(3, CX, LANES)

    def flat(values):
        return values.reshape(1, -1)

    openings = [flat(open_row), flat(open_col), flat(open_owner), flat(open_valid), flat(open_conduct)]
    inputs = [parent_state, parent_depth, child_state, child_depth, child_wet, *openings]
    up, dn, side = call(
        "edges",
        edges_kernel,
        [tile16] * 3,
        inputs,
        scratch=[pltpu.VMEM(a.shape, a.dtype) for a in inputs] + [pltpu.SemaphoreType.DMA((16,))],
        reads=HBM,
        limit=53.89,
    )
    cols0, cols1 = swap(side, "tile", 0), swap(side, "tile", 1)
    row2, row_t2, index_s, index_a, gain, lower, fixed, door2, door_t2, room, face, reply, place = call(
        "setup",
        setup_kernel,
        [
            sds(SLOTS, LANES, dtype=bf16), sds(CX, 2 * SLOTS, dtype=bf16), sds(SLOTS, LANES, dtype=i32),
            sds(SLOTS, LANES, dtype=i32), grid, grid, grid, sds(SLOTS, LANES, dtype=bf16),
            sds(CX, 2 * SLOTS, dtype=bf16), rooms, grid, grid, sds(16, LANES, dtype=i32),
        ],
        [*openings, jnp.transpose(parent_anchor, (0, 2, 1))[0], door_rows, interior_state, interior_wet],
        scratch=(CX + 16, CX + 16, 16),
    )
    above0 = to_next(dn, "district")
    below0 = to_previous(up, "district")
    near = call(
        "near",
        near_kernel,
        [
            sds(2 * SLOTS, LANES, dtype=bf16), sds(CX, 4 * SLOTS, dtype=bf16), sds(2 * SLOTS, LANES, dtype=i32),
            sds(2 * SLOTS, LANES), sds(SLOTS, LANES, dtype=i32), grid, grid, sds(16, 2 * SLOTS, dtype=bf16),
        ],
        [cols0, cols1],
    )
    near, siblings = near[:4], near[4:]
    for step in range(STEPS):
        with_step = lambda *refs, step=step: send_kernel(step, *refs)
        if step == 0:
            args = [
                place, parent_state, parent_depth, child_state, child_depth, child_wet, above0, below0, cols0, cols1,
                reply, row2, index_s,
            ]
            scratch = (CX + 16,) * 3 + (PX + 16,) * 3
        else:
            args = [
                place, parent_depth, child_depth, child_wet, above0, below0, cols0, cols1, reply, row2, index_s,
                moved, swapped, eta, u, v, v_h, eta_h, peta, pu, pv, pv_h, peta_h,
            ]
            scratch = (CX + 16,) * 2 + (PX + 16,) * 2
        outs = [block, tall, block, pblock, ptall, pblock, grid, sds(TILES, CAP if step == STEPS - 1 else 2 * CAP, LANES)]
        if step < STEPS - 1:
            outs += [block, pblock]
        eta, u, v, peta, pu, pv, street, outbox, *more = call(f"send{step}", with_step, outs, args, scratch=scratch)
        inbox = lax.all_to_all(outbox, "tile", split_axis=0, concat_axis=0, tiled=True)
        shared = [inbox, eta, street, row_t2, index_a, gain, lower]
        if step == STEPS - 1:
            return tuple(
                call(
                    "final",
                    final_kernel,
                    [sds(3, PX, LANES), rooms, rooms],
                    shared + [u, v, peta, pu, pv, room, face, door_t2],
                    scratch=(CX, CX, pltpu.SemaphoreType.DMA((9,))),
                    writes=HBM,
                )
            )
        v_h, pv_h = more
        eta, message, windows = call(
            f"street{step}", street_kernel, [block, tile8, tile8], [*shared, peta, *siblings]
        )
        moved = snake(message)
        with_step = lambda *refs, step=step: room_kernel(step + 1, *refs)
        room, face, reply, eta_h, peta_h = call(
            f"room{step}",
            with_step,
            [rooms, grid, grid, block, pblock],
            [inbox, windows, room, interior_wet, face, door2, door_t2, fixed, *near],
            scratch=(CX + 16, CX + 16),
        )
        moved, reply = lax.optimization_barrier((moved, reply))
        swapped = swap(moved, "tile", 0)


def solution(mesh):
    return jax.shard_map(
        body,
        mesh=mesh,
        in_specs=(
            P(None, "district", "tile"),
            P("district", "tile"),
            P(None, "district", "tile"),
            P("district", "tile"),
            P(None, "district", "tile"),
            P(None, ("district", "tile"), None),
            P(None, ("district", "tile"), None),
            P("district", None, None),
            P(("district", "tile")),
            P(("district", "tile")),
            P(("district", "tile"), None),
            P(("district", "tile")),
            P(("district", "tile")),
            P(("district", "tile"), None),
        ),
        out_specs=(
            P(None, "district", "tile"),
            P(None, "district", "tile"),
            P(None, ("district", "tile"), None),
        ),
        check_vma=False,
    )
```
